32 devices in a mesh: gx: 4 (over x, core), gy: 2 (over y), gz: 4 (over z).
Axes of the slice: x: 2, y: 2, z: 4, core: 2. Of those that a mesh axis runs over, the one named last changes fastest.
Arguments:
- spline_weights: bfloat16 [256, 256, 128], P(('gx', 'gy', 'gz')), may hold values from 0 to 0.125
- point_source: float32 [256, 256], P(('gx', 'gy', 'gz')), may hold values from -6 to 6
- confidence: float32 [256, 256], P(('gx', 'gy', 'gz')), may hold values from 0.25 to 4
- block_dest: int32 [256, 1], P(('gx', 'gy', 'gz')), may hold values from 0 to 7; in each aligned block of 8 rows (0 to 7, 8 to 15, ...) at most 2 rows name the same one
- offsets: int32 [3, 256], P(None, ('gx', 'gy', 'gz')), may hold values from 0 to 120, as said below
- block_count: int32 [32], P(('gx', 'gy', 'gz')), may hold values from 4 to 8, as said below
Outputs:
- solution_field: float32 [32, 16, 512], P('gx', 'gy', 'gz')
- residual: float32 [32, 16, 512], P('gx', 'gy', 'gz')
- point_field: float32 [256, 256], P(('gx', 'gy', 'gz'))
The draws below stay inside these ranges and needn't reach their ends.
Inputs may be any that keep to these rules, and one draw needn't show every extreme that they name: `block_dest`: among the 8 slots of each device at most 2 name one brick, a bound that some block reaches of them. `offsets`: rows 0, 1 and 2 lie in 0 to 4, 0 to 4, 0 to 120, so a patch never leaves its brick; each end is reached. `block_count`: some device has all 8 slots live.
All inputs are finite; a program needn't handle non-finite values.
Results may differ from the reference program's by a relative error of at most 0.0003.
Values sent between devices are 32-bit elements; how exact they have to be, the bound alone decides.
A program may use at most 64 MiB of HBM per device.

```python
import math
import jax
import jax.numpy as jnp
import numpy as np
from jax import lax

BX = 8
BY = 8
BZ = 128
PTS = 256
PX = 4
PY = 4
PZ = 8
ITERS = 3
NB = 8
PATCH = 128
CAP = 2
NBT = 256
NX = 32
NY = 16
NZ = 512
N_GY = 2
N_GZ = 4


def draw_offsets(key, part):
    key_x = jax.random.fold_in(key, 11)
    key_y = jax.random.fold_in(key, 12)
    key_z = jax.random.fold_in(key, 13)
    off_x = jax.random.randint(key_x, (NBT,), 0, BX - PX + 1, dtype=jnp.int32)
    off_y = jax.random.randint(key_y, (NBT,), 0, BY - PY + 1, dtype=jnp.int32)
    off_z = jax.random.randint(key_z, (NBT,), 0, BZ - PZ + 1, dtype=jnp.int32)
    stacked = jnp.stack([off_x, off_y, off_z], 0)
    ends = jnp.array([BX - PX, BY - PY, BZ - PZ], dtype=jnp.int32)
    stacked = stacked.at[:, 0].set(ends)
    stacked = stacked.at[:, 1].set(jnp.zeros((3,), jnp.int32))
    return stacked


def draw_block_count(key, part):
    devs = NBT // NB
    key_count = jax.random.fold_in(key, 21)
    key_full = jax.random.fold_in(key, 22)
    counts = jax.random.randint(key_count, (devs,), max(1, NB // 2), NB + 1, dtype=jnp.int32)
    chosen = jax.random.randint(key_full, (), 0, devs, dtype=jnp.int32)
    return counts.at[chosen].set(NB)


def level_of(stream_key, dims, split, smallest, top_value):
    level = 1.0
    for dim, shards_of in split:
        heights = jax.random.uniform(jax.random.fold_in(jax.random.fold_in(stream_key, 6), dim), (shards_of,), jnp.float32, smallest / len(split), top_value / len(split))
        level = level * jnp.repeat(jnp.exp(heights), dims[dim] // shards_of).reshape((-1,) + (1,) * (len(dims) - 1 - dim))
    return level


def routed_block(own_key, own, number, rows, count, top, bound, skew):
    ranking = jax.random.permutation(own_key, count)
    packed, usual = shares(count, rows * top, bound, skew, True), shares(count, rows * top, bound, skew, False)
    places = jnp.arange(count)

    def named(sizes, rotation):
        used = int((sizes > 0).sum())
        fixed = max(1, used // 4)
        shifted = fixed + (places - fixed + rotation * (used - fixed)) % max(1, count - fixed)
        return jnp.zeros((count,), jnp.int32).at[ranking[jnp.where(places < fixed, places, shifted)]].set(jnp.asarray(sizes, jnp.int32))

    sizes = jnp.where(number % 4 == 0, named(packed, number // 4), named(usual, number - number // 4 - 1))
    mixed = jax.random.permutation(jax.random.fold_in(own, 3), count)
    donor, sink = mixed[0:count // 2 * 2:2], mixed[1:count // 2 * 2:2]
    margin = jnp.minimum(sizes[donor] - 1, bound - sizes[sink]) // 2
    margin = jnp.where((donor == ranking[0]) | (sink == ranking[0]) | (sizes[sink] == 0), 0, jnp.maximum(margin, 0))
    shifted = jax.random.randint(jax.random.fold_in(own, 4), (count // 2,), 0, 1 << 20) % (margin + 1)
    sizes = sizes.at[donor].add(-shifted).at[sink].add(shifted)
    items = jnp.searchsorted(jnp.cumsum(sizes), jnp.arange(rows * top), side="right").astype(jnp.int32)
    listing = items.reshape(top, rows).T
    listing = listing[jax.random.permutation(jax.random.fold_in(own, 1), rows)]
    rotation = jax.random.randint(jax.random.fold_in(own, 2), (rows, 1), 0, top)
    return jnp.take_along_axis(listing, (jnp.arange(top)[None, :] + rotation) % top, axis=1)


def shares(number_of, total, limit, slope, full):
    loads = [(1 << 20) // math.isqrt(standing ** slope) + 1 for standing in range(1, number_of + 1)]
    largest = limit if full else min(limit, max(-(-total // number_of), total * loads[0] // sum(loads)))
    least = 1 if total - largest >= number_of - 1 else 0
    given, rest = [largest] + [least] * (number_of - 1), total - largest - least * (number_of - 1)
    while rest > 0:
        free = [i for i in range(1, number_of) if given[i] < largest] or [i for i in range(1, number_of) if given[i] < limit]
        mass, budget = sum([loads[i] for i in free]), rest
        for i in free:
            extra = min(limit - given[i], max(1, budget * loads[i] // mass), rest)
            given[i] = given[i] + extra
            rest = rest - extra
    return np.array(given)


def scatter_about(rng, dims, width, limit, shards=(), kind=jnp.bfloat16):
    entries = width * jax.random.normal(rng, dims, jnp.float32)
    if shards:
        entries = entries * level_of(rng, dims, shards, -0.22, 0.18)
    return jnp.clip(entries, -limit, limit).astype(kind)


def setup_inputs(seed: int = 0) -> dict:
    seeds = jax.random.split(jax.random.key(seed), 7)
    spline_weights = jnp.clip(0.125 * jax.random.uniform(seeds[0], (NBT, PTS, PATCH), jnp.float32) ** level_of(seeds[0], (NBT, PTS, PATCH), ((0, 32),), -0.2, 0.2), 0.0, 0.125).astype(jnp.bfloat16)
    point_source = scatter_about(seeds[1], (NBT, PTS), 1.0, 6.0, ((0, 32),), jnp.float32)
    confidence = jnp.clip(jnp.exp(math.log(4.0) - 2.7725887 * jax.random.uniform(seeds[2], (NBT, PTS), jnp.float32) ** level_of(seeds[2], (NBT, PTS), ((0, 32),), -0.2, 0.2)), 0.25, 4.0)
    block_dest_keys = jax.random.split(jax.random.fold_in(seeds[3], 1), NBT // NB)
    block_dest_turns = jax.random.permutation(jax.random.fold_in(seeds[3], 3), NBT // NB)
    block_dest = jax.vmap(lambda own, number: routed_block(jax.random.fold_in(seeds[3], 2), own, number, NB, N_GY * N_GZ, 1, CAP, 2))(block_dest_keys, block_dest_turns).reshape((NBT, 1))
    offsets = draw_offsets(jax.random.fold_in(seeds[6], 71), 0)
    block_count = draw_block_count(jax.random.fold_in(seeds[6], 71), 0)
    return {"spline_weights": spline_weights, "point_source": point_source, "confidence": confidence, "block_dest": block_dest, "offsets": offsets, "block_count": block_count}


def operate(field, center):
    padded = jnp.pad(field, 1)
    total = center * field
    sx, sy, sz = field.shape
    for dx in (-1, 0, 1):
        for dy in (-1, 0, 1):
            for dz in (-1, 0, 1):
                nonzero = abs(dx) + abs(dy) + abs(dz)
                if nonzero == 0:
                    continue
                weight = 0.5 ** (nonzero - 1)
                total = total - weight * padded[1 + dx:1 + dx + sx, 1 + dy:1 + dy + sy, 1 + dz:1 + dz + sz]
    return total


def reference(spline_weights, point_source, confidence, block_dest, offsets, block_count):
    group = N_GY * N_GZ
    devs = NBT // NB
    blocks = jnp.arange(NBT, dtype=jnp.int32)
    device = blocks // NB
    live = (blocks % NB) < block_count[device]
    slab = device // group
    dest = block_dest[:, 0]
    col_y = dest // N_GZ
    col_z = dest % N_GZ
    base = (slab * BX + offsets[0]) * (NY * NZ) + (col_y * BY + offsets[1]) * NZ + (col_z * BZ + offsets[2])
    cellno = jnp.arange(PATCH, dtype=jnp.int32)
    rel = (cellno // (PY * PZ)) * (NY * NZ) + ((cellno // PZ) % PY) * NZ + cellno % PZ
    index = (base[:, None] + rel[None, :]).astype(jnp.int32)
    weights_dev = spline_weights.reshape(devs, NB, PTS, PATCH)
    source_dev = point_source.reshape(devs, NB, PTS)
    conf_dev = confidence.reshape(devs, NB, PTS)

    def splat(item):
        wmat, src, conf = item
        wf = wmat.astype(jnp.float32)
        rhs_part = jnp.einsum("nps,np->ns", wf, src, precision=lax.Precision.HIGHEST)
        dens_part = jnp.einsum("nps,np->ns", wf * wf, conf, precision=lax.Precision.HIGHEST)
        return rhs_part, dens_part

    rhs_p, dens_p = lax.map(splat, (weights_dev, source_dev, conf_dev))
    livef = live.astype(jnp.float32)[:, None]
    rhs_p = rhs_p.reshape(NBT, PATCH) * livef
    dens_p = dens_p.reshape(NBT, PATCH) * livef
    cells = NX * NY * NZ
    rhs = jnp.zeros((cells,), jnp.float32).at[index.ravel()].add(rhs_p.ravel()).reshape(NX, NY, NZ)
    density = jnp.zeros((cells,), jnp.float32).at[index.ravel()].add(dens_p.ravel()).reshape(NX, NY, NZ)
    center = 14.0 + 4.0 * density
    solution_field = jnp.zeros_like(rhs)
    residual, direction = rhs, rhs
    norm_now = jnp.sum(residual * residual)
    for step in range(ITERS):
        image = operate(direction, center)
        alpha = norm_now / jnp.sum(direction * image)
        solution_field = solution_field + alpha * direction
        residual = residual - alpha * image
        norm_next = jnp.sum(residual * residual)
        direction = residual + (norm_next / norm_now) * direction
        norm_now = norm_next
    values = solution_field.ravel()[index].reshape(devs, NB, PATCH)

    def evaluate(item):
        wmat, vals = item
        return jnp.einsum("nps,ns->np", wmat.astype(jnp.float32), vals, precision=lax.Precision.HIGHEST)

    point_field = lax.map(evaluate, (weights_dev, values)).reshape(NBT, PTS) * livef
    return solution_field, residual, point_field
```

```python
import functools
import jax
import jax.numpy as jnp
from jax import lax
from jax.experimental import pallas as pl
from jax.experimental.pallas import tpu as pltpu
from jax.sharding import PartitionSpec as P

BX = 8
BY = 8
BZ = 128
PX = 4
PY = 4
PZ = 8
ITERS = 3
MESH = pl.DeviceIdType.MESH
F32 = jnp.float32
BF16 = jnp.bfloat16
HI = lax.Precision.HIGHEST
DIRS = [
    (dx, dy, dz)
    for dx in (-1, 0, 1)
    for dy in (-1, 0, 1)
    for dz in (-1, 0, 1)
    if (dx, dy, dz) != (0, 0, 0)
]


def code(dx, dy, dz):
    return (dx + 1) * 9 + (dy + 1) * 3 + (dz + 1)


def halves(value):
    high = value.astype(BF16)
    return high, (value - high.astype(F32)).astype(BF16)


def iota(shape, dim):
    return lax.broadcasted_iota(jnp.int32, shape, dim)


def repeat(count, body, init):
    if count <= 8:
        for i in range(count):
            init = body(i, init)
        return init
    return lax.fori_loop(0, count, body, init)


def smooth(v):
    n = v.shape[0]
    v = v[1 : n - 1] + 0.5 * (v[: n - 2] + v[2:])
    v = v + 0.5 * (pltpu.roll(v, 1, 1) + pltpu.roll(v, 15, 1))
    return v + 0.5 * (pltpu.roll(v, 1, 2) + pltpu.roll(v, 255, 2))


def coefficients(m):
    def add(p, a, q):
        out = []
        for i in range(max(len(p), len(q))):
            left = p[i] if i < len(p) else None
            right = a * q[i] if i < len(q) else None
            out.append(right if left is None else left if right is None else left + right)
        return out

    def form(p, q):
        total = None
        for i in range(len(p)):
            for j in range(len(q)):
                term = p[i] * q[j] * m[i + j]
                total = term if total is None else total + term
        return total

    one = jnp.ones_like(m[0])
    direction, residual, field = [one], [one], []
    now = m[0]
    for step in range(ITERS):
        image = [16.0 * c for c in direction] + [jnp.zeros_like(one)]
        image = [image[i] + (16.0 * direction[i - 1] if i else 0.0) for i in range(len(image))]
        alpha = now / form(direction, image)
        field = add(field, alpha, direction)
        residual = add(residual, -alpha, image)
        if step + 1 < ITERS:
            new = form(residual, residual)
            direction = add(residual, new / now, direction)
            now = new
    return field, residual


def kernel(sizes, w_hbm, src_hbm, conf_hbm, dest_hbm, off_hbm, count_hbm,
           field_ref, resid_ref, point_ref,
           send, recv, zhot, fbuf, ylow, yhigh, zpack, zrecv, yrecv, erecv, xrecv,
           part, parts, colpart, colparts, back, returned, pay, values_at,
           w_ref, src_ref, conf_ref, dest_ref, off_ref, in_s, h_s, h_r, one_s, one_r):
    nx, ny, nz, slots, cap = sizes
    group = ny * nz
    gx, gy, gz = lax.axis_index("gx"), lax.axis_index("gy"), lax.axis_index("gz")
    me = gy * nz + gz

    def ring(g, n):
        return [g] + [lax.rem(g + d, n) for d in range(1, n)]

    xs, ys, zs = ring(gx, nx), ring(gy, ny), ring(gz, nz)
    in_group = [(y * nz + z, (gx, y, z)) for y in ys for z in zs][1:]
    in_column = [(x, (x, gy, gz)) for x in xs][1:]
    everyone = [((x * ny + y) * nz + z, (x, y, z)) for x in xs for y in ys for z in zs][1:]

    def spread(kind, peers, src_of, dst, slot):
        copies = []
        for other, where in peers:
            c = pltpu.make_async_remote_copy(
                src_ref=src_of(other), dst_ref=dst.at[slot], send_sem=one_s.at[kind], recv_sem=one_r.at[kind],
                device_id=where, device_id_type=MESH,
            )
            c.start()
            copies.append(c)

    def whole(kind, peers, dst):
        ref = dst.at[pl.ds(0, len(peers))]
        return pltpu.make_async_remote_copy(
            src_ref=ref, dst_ref=ref, send_sem=one_s.at[kind], recv_sem=one_r.at[kind],
            device_id=peers[0][1], device_id_type=MESH,
        )

    def exists(dx, dy, dz):
        ok = None
        for d, g, n in ((dx, gx, nx), (dy, gy, ny), (dz, gz, nz)):
            if d:
                this = g + 1 < n if d > 0 else g > 0
                ok = this if ok is None else jnp.logical_and(ok, this)
        return ok

    loads = [
        pltpu.make_async_copy(a, b, in_s.at[i])
        for i, (a, b) in enumerate(
            (
                (dest_hbm, dest_ref), (off_hbm, off_ref),
                (src_hbm, src_ref), (conf_hbm, conf_ref), (w_hbm, w_ref),
            )
        )
    ]
    for c in loads:
        c.start()
    zrecv[...] = jnp.zeros_like(zrecv)
    yrecv[...] = jnp.zeros_like(yrecv)
    erecv[...] = jnp.zeros_like(erecv)
    xrecv[...] = jnp.zeros_like(xrecv)

    barrier = pltpu.get_barrier_semaphore()
    for _, where in in_group + in_column:
        pl.semaphore_signal(barrier, inc=1, device_id=where, device_id_type=MESH)

    for c in loads[:2]:
        c.wait()
    live_count = count_hbm[0]
    row_n, lane_n = iota((slots, slots), 0), iota((slots, slots), 1)
    eye = row_n == lane_n
    drow = dest_ref[...].astype(F32)
    dcol = jnp.sum(jnp.where(eye, drow, 0.0), axis=1, keepdims=True)
    earlier = (dcol == drow) & (lane_n < row_n) & (lane_n < live_count)
    rank = jnp.sum(jnp.where(earlier, 1.0, 0.0), axis=1, keepdims=True)
    tcol = jnp.where(iota((slots, 1), 0) < live_count, dcol * cap + rank, -1.0)
    off = off_ref[...].astype(F32)
    zcol = jnp.sum(jnp.where(eye, off[2:3], 0.0), axis=1, keepdims=True)
    xycol = jnp.sum(jnp.where(eye, off[0:1] * BY + off[1:2], 0.0), axis=1, keepdims=True)
    pay[2 * slots : 3 * slots, :] = jnp.broadcast_to(zcol, (slots, 128))
    pay[3 * slots : 4 * slots, :] = jnp.broadcast_to(xycol, (slots, 128))
    lanes = iota((slots, 4 * slots), 1)
    trow = jnp.sum(
        jnp.where(iota((slots, 4 * slots), 0) == lax.rem(lanes, slots), tcol, 0.0), axis=0, keepdims=True
    )
    rows = 4 * cap
    tr = iota((group * rows, 4 * slots), 0)
    tl = iota((group * rows, 4 * slots), 1)
    inner = lax.rem(tr, rows)
    want = (lax.div(tr, rows) * cap + lax.rem(inner, cap)).astype(F32)
    sel = jnp.where((lax.div(inner, cap) == lax.div(tl, slots)) & (want == trow), 1.0, 0.0)
    for c in loads[2:]:
        c.wait()
    s_hi, s_lo = halves(src_ref[...])
    c_hi, c_lo = halves(conf_ref[...])
    left_s = jnp.concatenate([s_hi, s_lo], 0)
    left_c = jnp.concatenate([c_hi, c_lo], 0)
    for n in range(slots):
        w = w_ref[n]
        wf = w.astype(F32)
        q_hi, q_lo = halves(wf * wf)
        rhs = jnp.dot(left_s, w, preferred_element_type=F32)
        den = jnp.dot(left_c, q_hi, preferred_element_type=F32) + jnp.dot(
            left_c, q_lo, preferred_element_type=F32
        )
        pay[n : n + 1, :] = rhs[n : n + 1] + rhs[slots + n : slots + n + 1]
        pay[slots + n : slots + n + 1, :] = den[n : n + 1] + den[slots + n : slots + n + 1]

    send[...] = jnp.dot(sel, pay[...], precision=HI, preferred_element_type=F32).reshape(group, rows, 128)
    recv[me] = send[me]

    pl.semaphore_wait(barrier, len(in_group) + len(in_column))
    spread(0, in_group, lambda other: send.at[other], recv, me)
    whole(0, in_group, recv).wait_recv()

    cell = iota((BX * BY, 128), 1)
    place_xy = (iota((BX * BY, 128), 0) - (lax.shift_right_logical(cell, 5) * BY + (lax.shift_right_logical(cell, 3) & 3))).astype(F32)
    place_z = (iota((128, BZ), 1) - (iota((128, BZ), 0) & 7)).astype(F32)

    def scatter(g, acc):
        got = recv[g]
        lefts, hots = [], []
        for k in range(cap):
            hot = jnp.where(place_z == got[2 * cap + k : 2 * cap + k + 1], 1.0, 0.0).astype(BF16)
            hots.append(hot)
            at = place_xy == got[3 * cap + k : 3 * cap + k + 1]
            values = jnp.concatenate(
                [jnp.where(at, got[k : k + 1], 0.0), jnp.where(at, got[cap + k : cap + k + 1], 0.0)], 0
            )
            lefts.append(jnp.concatenate(halves(values), 0))
        hot = jnp.concatenate(hots, 0)
        zhot[g] = hot
        return acc + jnp.dot(jnp.concatenate(lefts, 1), hot, preferred_element_type=F32)

    acc = repeat(group, scatter, jnp.zeros((4 * BX * BY, BZ), F32))
    both = acc[: 2 * BX * BY] + acc[2 * BX * BY :]
    rhs = both[: BX * BY].reshape(BX, BY, BZ)
    den = (0.25 * both[BX * BY :]).reshape(BX, BY, BZ)

    lane = iota((BY, BZ), 1)
    sub = iota((BY, BZ), 0)
    rim = (lane < 3) | (lane >= BZ - 3)
    packed = jnp.zeros((BY, BZ), F32)
    for f, field in enumerate((rhs, den)):
        for x in range(BX):
            edge = jnp.where(rim, field[x], 0.0)
            shift = 8 * x + 64 * f
            packed = packed + (pltpu.roll(edge, shift, 1) if shift else edge)
            fbuf[x, f] = field[x]
        for j in range(BX // 2):
            even, odd = field[2 * j], pltpu.roll(field[2 * j + 1], 4, 0)
            ylow[j, f] = jnp.where(sub < 4, even, odd)
            yhigh[j, f] = jnp.where(sub < 4, odd, even)
    zpack[...] = packed

    def buffers(dx, dy, dz):
        if dz:
            return zpack, zrecv.at[code(-dx, -dy, -dz)]
        if dy:
            source = ylow if dy < 0 else yhigh
            side = 0 if dy > 0 else 1
            if not dx:
                return source, yrecv.at[side]
            return source.at[pl.ds(2 if dx > 0 else 0, 2)], erecv.at[0 if dx > 0 else 1, side]
        return fbuf.at[pl.ds(5 if dx > 0 else 0, 3)], xrecv.at[0 if dx > 0 else 1]

    def halo(dx, dy, dz):
        source, target = buffers(dx, dy, dz)
        return pltpu.make_async_remote_copy(
            src_ref=source, dst_ref=target,
            send_sem=h_s.at[code(dx, dy, dz)], recv_sem=h_r.at[code(-dx, -dy, -dz)],
            device_id=(gx + dx, gy + dy, gz + dz), device_id_type=MESH,
        )

    order = sorted(DIRS, key=lambda d: (d[2] != 0, d[0] != 0))
    for d in order:
        @pl.when(exists(*d))
        def _():
            halo(*d).start()
    whole(0, in_group, recv).wait_send()
    for d in order:
        @pl.when(exists(*d))
        def _():
            dx, dy, dz = d
            halo(-dx, -dy, -dz).wait_recv()

    def rim_pack(dx, dy):
        return jnp.where((lane & 7) < 4, zrecv[code(dx, dy, 1)], zrecv[code(dx, dy, -1)])

    fields = [[], []]
    for dx, xs in ((-1, (5, 6, 7)), (0, tuple(range(BX))), (1, (0, 1, 2))):
        pack0 = rim_pack(dx, 0)
        pack1 = jnp.where(sub < 4, rim_pack(dx, 1), rim_pack(dx, -1))
        for i, x in enumerate(xs):
            for f in range(2):
                if dx:
                    side = 0 if dx < 0 else 1
                    own = xrecv[side, i, f]
                    pair = x // 2 - (2 if dx < 0 else 0)
                    low, high = erecv[side, 1, pair, f], erecv[side, 0, pair, f]
                else:
                    own = fbuf[x, f]
                    low, high = yrecv[1, x // 2, f], yrecv[0, x // 2, f]
                if x % 2 == 0:
                    beside = jnp.where(sub < 4, low, high)
                else:
                    beside = pltpu.roll(jnp.where(sub < 4, high, low), 4, 0)
                shift = (BZ - 8 * x - 64 * f) % BZ
                z0 = jnp.where(rim, pltpu.roll(pack0, shift, 1) if shift else pack0, 0.0)
                z1 = jnp.where(rim, pltpu.roll(pack1, shift, 1) if shift else pack1, 0.0)
                top = jnp.concatenate([own, z0], 1)
                low_rows = jnp.concatenate([beside, z1], 1)
                fields[f].append(jnp.concatenate([top, low_rows], 0))
    v0, dens = jnp.stack(fields[0]), jnp.stack(fields[1])

    ry, rz = iota((16, 256), 0), iota((16, 256), 1)
    yes = ((ry < 8) | ((ry < 12) & (gy + 1 < ny)) | ((ry >= 12) & (gy > 0))) & (
        (rz < 128) | ((rz < 192) & (gz + 1 < nz)) | ((rz >= 192) & (gz > 0))
    )
    inside = jnp.where(yes, 1.0, 0.0)
    before = inside * jnp.where(gx > 0, 1.0, 0.0)
    after = inside * jnp.where(gx + 1 < nx, 1.0, 0.0)

    def step(v, depth):
        out = dens[depth : 14 - depth] * v[1:-1] - 0.125 * smooth(v)
        rims = 3 - depth
        masks = [before] * rims + [inside] * BX + [after] * rims
        return out * jnp.stack(masks) if rims else out

    v1 = step(v0, 1)
    v2 = step(v1, 2)
    v3 = step(v2, 3)
    basis = [rhs, v1[2:10, :8, :128], v2[1:9, :8, :128], v3[:, :8, :128]]
    lines = []
    for k in range(2 * ITERS):
        product = jnp.sum(basis[k // 2] * basis[(k + 1) // 2], axis=0)
        lines.append(jnp.sum(product, axis=0, keepdims=True))
    lines.append(jnp.zeros((2, 128), F32))
    fold = jnp.concatenate(lines, 0)
    for shift in (64, 32, 16):
        fold = fold + pltpu.roll(fold, shift, 1)
    own = lax.shift_right_logical(lane, 4) == sub

    direct = nx * group <= 64
    peers = everyone if direct else in_group
    spot = gx * group + me if direct else me
    line = jnp.sum(jnp.where(own, fold, 0.0), axis=0, keepdims=True)
    part[...] = line
    parts[spot] = line
    spread(1, peers, lambda other: part, parts, spot)

    flat = jnp.concatenate(halves(jnp.concatenate([v.reshape(BX * BY, BZ) for v in basis[:ITERS]], 0)), 0)
    tall = ITERS * BX * BY

    def gather(g, carry):
        picked = lax.dot_general(flat, zhot[g], (((1,), (1,)), ((), ())), preferred_element_type=F32)
        picked = picked[:tall] + picked[tall:]
        got = recv[g]
        at = [place_xy == got[3 * cap + k : 3 * cap + k + 1] for k in range(cap)]
        lines = []
        for v in range(ITERS):
            for k in range(cap):
                cells = picked[BX * BY * v : BX * BY * (v + 1), 128 * k : 128 * k + 128]
                lines.append(jnp.sum(jnp.where(at[k], cells, 0.0), axis=0, keepdims=True))
        lines.append(jnp.zeros((rows - ITERS * cap, 128), F32))
        back[g] = jnp.concatenate(lines, 0)
        return carry

    repeat(group, gather, 0)
    returned[me] = back[me]
    spread(2, in_group, lambda other: back.at[other], returned, me)
    for d in order:
        @pl.when(exists(*d))
        def _():
            halo(*d).wait_send()
    tr = iota((slots, group * rows), 1)
    inner = lax.rem(tr, rows)
    want = (lax.div(tr, rows) * cap + lax.rem(inner, cap)).astype(F32)
    sel = jnp.concatenate(
        [jnp.where((lax.div(inner, cap) == v) & (want == tcol), 1.0, 0.0) for v in range(ITERS)], 0
    )
    whole(2, in_group, returned).wait_recv()
    values = jnp.dot(sel, returned[...].reshape(group * rows, 128), precision=HI, preferred_element_type=F32)
    left = jnp.concatenate(halves(values), 0)
    for n in range(slots):
        out = lax.dot_general(left, w_ref[n], (((1,), (1,)), ((), ())), preferred_element_type=F32)
        for v in range(ITERS):
            at = v * slots + n
            values_at[v, n : n + 1, :] = out[at : at + 1] + out[ITERS * slots + at : ITERS * slots + at + 1]

    whole(1, peers, parts).wait_recv()
    total = repeat(len(peers) + 1, lambda g, t: t + parts[g], jnp.zeros((1, 128), F32))
    if not direct:
        colpart[...] = total
        colparts[gx] = total
        spread(3, in_column, lambda other: colpart, colparts, gx)
        whole(3, in_column, colparts).wait_recv()
        total = repeat(nx, lambda g, t: t + colparts[g], jnp.zeros((1, 128), F32))
    total = jnp.where(own, jnp.broadcast_to(total, (8, 128)), 0.0)
    moments = jnp.broadcast_to(jnp.sum(total, axis=1, keepdims=True), (8, 128))
    field_c, resid_c = coefficients([moments[k : k + 1] for k in range(2 * ITERS)])

    def combine(cs):
        out = None
        for c, v in zip(cs, basis):
            term = c.reshape(1, 1, 128) * v
            out = term if out is None else out + term
        return out

    field_ref[...] = combine(field_c)
    resid_ref[...] = combine(resid_c)
    point = None
    for v, c in enumerate(field_c):
        term = jnp.concatenate([c] * (values_at.shape[2] // 128), 1) * values_at[v]
        point = term if point is None else point + term
    point_ref[...] = point
    whole(1, peers, parts).wait_send()
    whole(2, in_group, returned).wait_send()
    if not direct:
        whole(3, in_column, colparts).wait_send()


def shards(nx, ny, nz, spline_weights, point_source, confidence, block_dest, offsets, block_count):
    slots, points, patch = spline_weights.shape
    group = ny * nz
    cap = max(2, (slots + group - 1) // group)
    rows = 4 * cap
    vmem = pl.BlockSpec(memory_space=pltpu.VMEM)
    dma = pltpu.SemaphoreType.DMA
    return pl.pallas_call(
        functools.partial(kernel, (nx, ny, nz, slots, cap)),
        out_shape=(
            jax.ShapeDtypeStruct((BX, BY, BZ), F32),
            jax.ShapeDtypeStruct((BX, BY, BZ), F32),
            jax.ShapeDtypeStruct((slots, points), F32),
        ),
        in_specs=[pl.BlockSpec(memory_space=pltpu.HBM)] * 5 + [pl.BlockSpec(memory_space=pltpu.SMEM)],
        out_specs=(vmem, vmem, vmem),
        scratch_shapes=[
            pltpu.VMEM((group, rows, 128), F32),
            pltpu.VMEM((group, rows, 128), F32),
            pltpu.VMEM((group, cap * 128, BZ), BF16),
            pltpu.VMEM((BX, 2, BY, BZ), F32),
            pltpu.VMEM((BX // 2, 2, BY, BZ), F32),
            pltpu.VMEM((BX // 2, 2, BY, BZ), F32),
            pltpu.VMEM((BY, BZ), F32),
            pltpu.VMEM((27, BY, BZ), F32),
            pltpu.VMEM((2, BX // 2, 2, BY, BZ), F32),
            pltpu.VMEM((2, 2, 2, 2, BY, BZ), F32),
            pltpu.VMEM((2, 3, 2, BY, BZ), F32),
            pltpu.VMEM((1, 128), F32),
            pltpu.VMEM((nx * group, 1, 128), F32),
            pltpu.VMEM((1, 128), F32),
            pltpu.VMEM((nx, 1, 128), F32),
            pltpu.VMEM((group, rows, 128), F32),
            pltpu.VMEM((group, rows, 128), F32),
            pltpu.VMEM((4 * slots, 128), F32),
            pltpu.VMEM((ITERS, slots, points), F32),
            pltpu.VMEM(spline_weights.shape, BF16),
            pltpu.VMEM(point_source.shape, F32),
            pltpu.VMEM(confidence.shape, F32),
            pltpu.VMEM((1, slots), jnp.int32),
            pltpu.VMEM(offsets.shape, jnp.int32),
            dma((6,)), dma((27,)), dma((27,)), dma((4,)), dma((4,)),
        ],
        compiler_params=pltpu.CompilerParams(
            collective_id=0, has_side_effects=True, vmem_limit_bytes=40 * 1024 * 1024
        ),
    )(
        *(
            pltpu.with_memory_space_constraint(a, pltpu.HBM)
            for a in (
                spline_weights, point_source, confidence, block_dest.reshape(1, slots), offsets,
            )
        ),
        block_count.reshape((1,)),
    )


def solution(mesh):
    sizes = (mesh.shape["gx"], mesh.shape["gy"], mesh.shape["gz"])
    return jax.shard_map(
        functools.partial(shards, *sizes),
        mesh=mesh,
        in_specs=(
            P(("gx", "gy", "gz"), None, None),
            P(("gx", "gy", "gz"), None),
            P(("gx", "gy", "gz"), None),
            P(("gx", "gy", "gz"), None),
            P(None, ("gx", "gy", "gz")),
            P(("gx", "gy", "gz")),
        ),
        out_specs=(P("gx", "gy", "gz"), P("gx", "gy", "gz"), P(("gx", "gy", "gz"), None)),
        check_vma=False,
    )
```

```python
import functools
import jax
import jax.numpy as jnp
from jax import lax
from jax.experimental import pallas as pl
from jax.experimental.pallas import tpu as pltpu
from jax.sharding import PartitionSpec as P

BX = 8
BY = 8
BZ = 128
PX = 4
PY = 4
PZ = 8
ITERS = 3
MESH = pl.DeviceIdType.MESH
F32 = jnp.float32
BF16 = jnp.bfloat16
HI = lax.Precision.HIGHEST
DIRS = [
    (dx, dy, dz)
    for dx in (-1, 0, 1)
    for dy in (-1, 0, 1)
    for dz in (-1, 0, 1)
    if (dx, dy, dz) != (0, 0, 0)
]


def code(dx, dy, dz):
    return (dx + 1) * 9 + (dy + 1) * 3 + (dz + 1)


def halves(value):
    high = value.astype(BF16)
    return high, (value - high.astype(F32)).astype(BF16)


def iota(shape, dim):
    return lax.broadcasted_iota(jnp.int32, shape, dim)


def repeat(count, body, init):
    if count <= 8:
        for i in range(count):
            init = body(i, init)
        return init
    return lax.fori_loop(0, count, body, init)


def smooth(v):
    n = v.shape[0]
    v = v[1 : n - 1] + 0.5 * (v[: n - 2] + v[2:])
    v = v + 0.5 * (pltpu.roll(v, 1, 1) + pltpu.roll(v, 15, 1))
    return v + 0.5 * (pltpu.roll(v, 1, 2) + pltpu.roll(v, 255, 2))


def coefficients(m):
    def add(p, a, q):
        out = []
        for i in range(max(len(p), len(q))):
            left = p[i] if i < len(p) else None
            right = a * q[i] if i < len(q) else None
            out.append(right if left is None else left if right is None else left + right)
        return out

    def form(p, q):
        total = None
        for i in range(len(p)):
            for j in range(len(q)):
                term = p[i] * q[j] * m[i + j]
                total = term if total is None else total + term
        return total

    one = jnp.ones_like(m[0])
    direction, residual, field = [one], [one], []
    now = m[0]
    for step in range(ITERS):
        image = [16.0 * c for c in direction] + [jnp.zeros_like(one)]
        image = [image[i] + (16.0 * direction[i - 1] if i else 0.0) for i in range(len(image))]
        alpha = now / form(direction, image)
        field = add(field, alpha, direction)
        residual = add(residual, -alpha, image)
        if step + 1 < ITERS:
            new = form(residual, residual)
            direction = add(residual, new / now, direction)
            now = new
    return field, residual


def kernel(sizes, w_hbm, src_hbm, conf_hbm, dest_hbm, off_hbm, count_hbm,
           basis_ref, values_at, sums_ref,
           send, recv, zhot, fbuf, ylow, yhigh, zpack, zrecv, yrecv, erecv, xrecv,
           part, parts, colpart, colparts, back, returned, pay,
           w_ref, src_ref, conf_ref, dest_ref, off_ref, in_s, h_s, h_r, one_s, one_r):
    nx, ny, nz, slots, cap = sizes
    group = ny * nz
    gx, gy, gz = lax.axis_index("gx"), lax.axis_index("gy"), lax.axis_index("gz")
    me = gy * nz + gz

    def ring(g, n):
        return [g] + [lax.rem(g + d, n) for d in range(1, n)]

    xs, ys, zs = ring(gx, nx), ring(gy, ny), ring(gz, nz)
    in_group = [(y * nz + z, (gx, y, z)) for y in ys for z in zs][1:]
    in_column = [(x, (x, gy, gz)) for x in xs][1:]
    everyone = [((x * ny + y) * nz + z, (x, y, z)) for x in xs for y in ys for z in zs][1:]

    def spread(kind, peers, src_of, dst, slot):
        copies = []
        for other, where in peers:
            c = pltpu.make_async_remote_copy(
                src_ref=src_of(other), dst_ref=dst.at[slot], send_sem=one_s.at[kind], recv_sem=one_r.at[kind],
                device_id=where, device_id_type=MESH,
            )
            c.start()
            copies.append(c)

    def whole(kind, peers, dst):
        ref = dst.at[pl.ds(0, len(peers))]
        return pltpu.make_async_remote_copy(
            src_ref=ref, dst_ref=ref, send_sem=one_s.at[kind], recv_sem=one_r.at[kind],
            device_id=peers[0][1], device_id_type=MESH,
        )

    def exists(dx, dy, dz):
        ok = None
        for d, g, n in ((dx, gx, nx), (dy, gy, ny), (dz, gz, nz)):
            if d:
                this = g + 1 < n if d > 0 else g > 0
                ok = this if ok is None else jnp.logical_and(ok, this)
        return ok

    loads = [
        pltpu.make_async_copy(a, b, in_s.at[i])
        for i, (a, b) in enumerate(
            (
                (dest_hbm, dest_ref), (off_hbm, off_ref),
                (src_hbm, src_ref), (conf_hbm, conf_ref), (w_hbm, w_ref),
            )
        )
    ]
    barrier = pltpu.get_barrier_semaphore()
    for _, where in reversed(in_group):
        pl.semaphore_signal(barrier, inc=1, device_id=where, device_id_type=MESH)
    for c in loads:
        c.start()
    zrecv[...] = jnp.zeros_like(zrecv)
    yrecv[...] = jnp.zeros_like(yrecv)
    erecv[...] = jnp.zeros_like(erecv)
    xrecv[...] = jnp.zeros_like(xrecv)

    for _, where in in_column:
        pl.semaphore_signal(barrier, inc=1, device_id=where, device_id_type=MESH)

    for c in loads[:2]:
        c.wait()
    live_count = count_hbm[0]
    row_n, lane_n = iota((slots, slots), 0), iota((slots, slots), 1)
    eye = row_n == lane_n
    drow = dest_ref[...].astype(F32)
    dcol = jnp.sum(jnp.where(eye, drow, 0.0), axis=1, keepdims=True)
    earlier = (dcol == drow) & (lane_n < row_n) & (lane_n < live_count)
    rank = jnp.sum(jnp.where(earlier, 1.0, 0.0), axis=1, keepdims=True)
    tcol = jnp.where(iota((slots, 1), 0) < live_count, dcol * cap + rank, -1.0)
    off = off_ref[...].astype(F32)
    zcol = jnp.sum(jnp.where(eye, off[2:3], 0.0), axis=1, keepdims=True)
    xycol = jnp.sum(jnp.where(eye, off[0:1] * BY + off[1:2], 0.0), axis=1, keepdims=True)
    pay[2 * slots : 3 * slots, :] = jnp.broadcast_to(zcol, (slots, 128))
    pay[3 * slots : 4 * slots, :] = jnp.broadcast_to(xycol, (slots, 128))
    lanes = iota((slots, 4 * slots), 1)
    trow = jnp.sum(
        jnp.where(iota((slots, 4 * slots), 0) == lax.rem(lanes, slots), tcol, 0.0), axis=0, keepdims=True
    )
    rows = 4 * cap
    tr = iota((group * rows, 4 * slots), 0)
    tl = iota((group * rows, 4 * slots), 1)
    inner = lax.rem(tr, rows)
    want = (lax.div(tr, rows) * cap + lax.rem(inner, cap)).astype(F32)
    sel = jnp.where((lax.div(inner, cap) == lax.div(tl, slots)) & (want == trow), 1.0, 0.0)
    for c in loads[2:]:
        c.wait()
    s_hi, s_lo = halves(src_ref[...])
    c_hi, c_lo = halves(conf_ref[...])
    left_s = jnp.concatenate([s_hi, s_lo], 0)
    left_c = jnp.concatenate([c_hi, c_lo], 0)
    for n in range(slots):
        w = w_ref[n]
        wf = w.astype(F32)
        q_hi, q_lo = halves(wf * wf)
        rhs = jnp.dot(left_s, w, preferred_element_type=F32)
        den = jnp.dot(left_c, q_hi, preferred_element_type=F32) + jnp.dot(
            left_c, q_lo, preferred_element_type=F32
        )
        pay[n : n + 1, :] = rhs[n : n + 1] + rhs[slots + n : slots + n + 1]
        pay[slots + n : slots + n + 1, :] = den[n : n + 1] + den[slots + n : slots + n + 1]

    send[...] = jnp.dot(sel, pay[...], precision=HI, preferred_element_type=F32).reshape(group, rows, 128)
    recv[me] = send[me]

    pl.semaphore_wait(barrier, len(in_group) + len(in_column))
    spread(0, in_group, lambda other: send.at[other], recv, me)
    whole(0, in_group, recv).wait_recv()

    cell = iota((BX * BY, 128), 1)
    place_xy = (iota((BX * BY, 128), 0) - (lax.shift_right_logical(cell, 5) * BY + (lax.shift_right_logical(cell, 3) & 3))).astype(F32)
    place_z = (iota((128, BZ), 1) - (iota((128, BZ), 0) & 7)).astype(F32)

    def scatter(g, acc):
        got = recv[g]
        lefts, hots = [], []
        for k in range(cap):
            hot = jnp.where(place_z == got[2 * cap + k : 2 * cap + k + 1], 1.0, 0.0).astype(BF16)
            hots.append(hot)
            at = place_xy == got[3 * cap + k : 3 * cap + k + 1]
            values = jnp.concatenate(
                [jnp.where(at, got[k : k + 1], 0.0), jnp.where(at, got[cap + k : cap + k + 1], 0.0)], 0
            )
            lefts.append(jnp.concatenate(halves(values), 0))
        hot = jnp.concatenate(hots, 0)
        zhot[g] = hot
        return acc + jnp.dot(jnp.concatenate(lefts, 1), hot, preferred_element_type=F32)

    acc = repeat(group, scatter, jnp.zeros((4 * BX * BY, BZ), F32))
    both = acc[: 2 * BX * BY] + acc[2 * BX * BY :]
    rhs = both[: BX * BY].reshape(BX, BY, BZ)
    den = (0.25 * both[BX * BY :]).reshape(BX, BY, BZ)

    lane = iota((BY, BZ), 1)
    sub = iota((BY, BZ), 0)
    rim = (lane < 3) | (lane >= BZ - 3)
    packed = jnp.zeros((BY, BZ), F32)
    for f, field in enumerate((rhs, den)):
        for x in range(BX):
            edge = jnp.where(rim, field[x], 0.0)
            shift = 8 * x + 64 * f
            packed = packed + (pltpu.roll(edge, shift, 1) if shift else edge)
            fbuf[x, f] = field[x]
        for j in range(BX // 2):
            even, odd = field[2 * j], pltpu.roll(field[2 * j + 1], 4, 0)
            ylow[j, f] = jnp.where(sub < 4, even, odd)
            yhigh[j, f] = jnp.where(sub < 4, odd, even)
    zpack[...] = packed

    def buffers(dx, dy, dz):
        if dz:
            return zpack, zrecv.at[code(-dx, -dy, -dz)]
        if dy:
            source = ylow if dy < 0 else yhigh
            side = 0 if dy > 0 else 1
            if not dx:
                return source, yrecv.at[side]
            return source.at[pl.ds(2 if dx > 0 else 0, 2)], erecv.at[0 if dx > 0 else 1, side]
        return fbuf.at[pl.ds(5 if dx > 0 else 0, 3)], xrecv.at[0 if dx > 0 else 1]

    def halo(dx, dy, dz):
        source, target = buffers(dx, dy, dz)
        return pltpu.make_async_remote_copy(
            src_ref=source, dst_ref=target,
            send_sem=h_s.at[code(dx, dy, dz)], recv_sem=h_r.at[code(-dx, -dy, -dz)],
            device_id=(gx + dx, gy + dy, gz + dz), device_id_type=MESH,
        )

    order = sorted(DIRS, key=lambda d: (d[2] != 0, d[0] != 0))
    for d in order:
        @pl.when(exists(*d))
        def _():
            halo(*d).start()
    whole(0, in_group, recv).wait_send()
    for d in order:
        @pl.when(exists(*d))
        def _():
            dx, dy, dz = d
            halo(-dx, -dy, -dz).wait_recv()

    def rim_pack(dx, dy):
        return jnp.where((lane & 7) < 4, zrecv[code(dx, dy, 1)], zrecv[code(dx, dy, -1)])

    fields = [[], []]
    for dx, xs in ((-1, (5, 6, 7)), (0, tuple(range(BX))), (1, (0, 1, 2))):
        pack0 = rim_pack(dx, 0)
        pack1 = jnp.where(sub < 4, rim_pack(dx, 1), rim_pack(dx, -1))
        for i, x in enumerate(xs):
            for f in range(2):
                if dx:
                    side = 0 if dx < 0 else 1
                    own = xrecv[side, i, f]
                    pair = x // 2 - (2 if dx < 0 else 0)
                    low, high = erecv[side, 1, pair, f], erecv[side, 0, pair, f]
                else:
                    own = fbuf[x, f]
                    low, high = yrecv[1, x // 2, f], yrecv[0, x // 2, f]
                if x % 2 == 0:
                    beside = jnp.where(sub < 4, low, high)
                else:
                    beside = pltpu.roll(jnp.where(sub < 4, high, low), 4, 0)
                shift = (BZ - 8 * x - 64 * f) % BZ
                z0 = jnp.where(rim, pltpu.roll(pack0, shift, 1) if shift else pack0, 0.0)
                z1 = jnp.where(rim, pltpu.roll(pack1, shift, 1) if shift else pack1, 0.0)
                top = jnp.concatenate([own, z0], 1)
                low_rows = jnp.concatenate([beside, z1], 1)
                fields[f].append(jnp.concatenate([top, low_rows], 0))
    v0, dens = jnp.stack(fields[0]), jnp.stack(fields[1])

    ry, rz = iota((16, 256), 0), iota((16, 256), 1)
    yes = ((ry < 8) | ((ry < 12) & (gy + 1 < ny)) | ((ry >= 12) & (gy > 0))) & (
        (rz < 128) | ((rz < 192) & (gz + 1 < nz)) | ((rz >= 192) & (gz > 0))
    )
    inside = jnp.where(yes, 1.0, 0.0)
    before = inside * jnp.where(gx > 0, 1.0, 0.0)
    after = inside * jnp.where(gx + 1 < nx, 1.0, 0.0)

    def step(v, depth):
        out = dens[depth : 14 - depth] * v[1:-1] - 0.125 * smooth(v)
        rims = 3 - depth
        masks = [before] * rims + [inside] * BX + [after] * rims
        return out * jnp.stack(masks) if rims else out

    v1 = step(v0, 1)
    v2 = step(v1, 2)
    v3 = step(v2, 3)
    basis = [rhs, v1[2:10, :8, :128], v2[1:9, :8, :128], v3[:, :8, :128]]
    basis_ref[0] = rhs
    lines = []
    for k in range(2 * ITERS):
        product = jnp.sum(basis[k // 2] * basis[(k + 1) // 2], axis=0)
        lines.append(jnp.sum(product, axis=0, keepdims=True))
    lines.append(jnp.zeros((2, 128), F32))
    fold = jnp.concatenate(lines, 0)
    for shift in (64, 32, 16):
        fold = fold + pltpu.roll(fold, shift, 1)
    own = lax.shift_right_logical(lane, 4) == sub

    direct = nx * group <= 64
    peers = everyone if direct else in_group
    spot = gx * group + me if direct else me
    line = jnp.sum(jnp.where(own, fold, 0.0), axis=0, keepdims=True)
    part[...] = line
    parts[spot] = line
    spread(1, peers, lambda other: part, parts, spot)
    for k in range(1, ITERS + 1):
        basis_ref[k] = basis[k]

    flat = jnp.concatenate(halves(jnp.concatenate([v.reshape(BX * BY, BZ) for v in basis[:ITERS]], 0)), 0)
    tall = ITERS * BX * BY

    def gather(g, carry):
        picked = lax.dot_general(flat, zhot[g], (((1,), (1,)), ((), ())), preferred_element_type=F32)
        picked = picked[:tall] + picked[tall:]
        got = recv[g]
        at = [place_xy == got[3 * cap + k : 3 * cap + k + 1] for k in range(cap)]
        lines = []
        for v in range(ITERS):
            for k in range(cap):
                cells = picked[BX * BY * v : BX * BY * (v + 1), 128 * k : 128 * k + 128]
                lines.append(jnp.sum(jnp.where(at[k], cells, 0.0), axis=0, keepdims=True))
        lines.append(jnp.zeros((rows - ITERS * cap, 128), F32))
        back[g] = jnp.concatenate(lines, 0)
        return carry

    repeat(group, gather, 0)
    returned[me] = back[me]
    spread(2, in_group, lambda other: back.at[other], returned, me)
    for d in order:
        @pl.when(exists(*d))
        def _():
            halo(*d).wait_send()
    tr = iota((slots, group * rows), 1)
    inner = lax.rem(tr, rows)
    want = (lax.div(tr, rows) * cap + lax.rem(inner, cap)).astype(F32)
    sel = jnp.concatenate(
        [jnp.where((lax.div(inner, cap) == v) & (want == tcol), 1.0, 0.0) for v in range(ITERS)], 0
    )
    whole(2, in_group, returned).wait_recv()
    values = jnp.dot(sel, returned[...].reshape(group * rows, 128), precision=HI, preferred_element_type=F32)
    left = jnp.concatenate(halves(values), 0)
    for n in range(slots):
        out = lax.dot_general(left, w_ref[n], (((1,), (1,)), ((), ())), preferred_element_type=F32)
        for v in range(ITERS):
            at = v * slots + n
            values_at[v, n : n + 1, :] = out[at : at + 1] + out[ITERS * slots + at : ITERS * slots + at + 1]

    whole(1, peers, parts).wait_recv()
    total = repeat(len(peers) + 1, lambda g, t: t + parts[g], jnp.zeros((1, 128), F32))
    if not direct:
        colpart[...] = total
        colparts[gx] = total
        spread(3, in_column, lambda other: colpart, colparts, gx)
        whole(3, in_column, colparts).wait_recv()
        total = repeat(nx, lambda g, t: t + colparts[g], jnp.zeros((1, 128), F32))
    sums_ref[...] = jnp.where(own, jnp.broadcast_to(total, (8, 128)), 0.0)
    whole(1, peers, parts).wait_send()
    whole(2, in_group, returned).wait_send()
    if not direct:
        whole(3, in_column, colparts).wait_send()


def finish(basis_ref, values_at, sums_ref, field_hbm, resid_hbm, point_hbm, field_ref, resid_ref, point_ref, out_s):
    moments = jnp.broadcast_to(jnp.sum(sums_ref[...], axis=1, keepdims=True), (8, 128))
    field_c, resid_c = coefficients([moments[k : k + 1] for k in range(2 * ITERS)])
    copies = [
        pltpu.make_async_copy(a, b, out_s.at[i])
        for i, (a, b) in enumerate(((field_ref, field_hbm), (point_ref, point_hbm), (resid_ref, resid_hbm)))
    ]

    def combine(cs):
        out = None
        for k, c in enumerate(cs):
            term = c.reshape(1, 1, 128) * basis_ref[k]
            out = term if out is None else out + term
        return out

    field_ref[...] = combine(field_c)
    copies[0].start()
    point = None
    for v, c in enumerate(field_c):
        term = jnp.concatenate([c] * (values_at.shape[2] // 128), 1) * values_at[v]
        point = term if point is None else point + term
    point_ref[...] = point
    copies[1].start()
    resid_ref[...] = combine(resid_c)
    copies[2].start()
    for c in copies:
        c.wait()


def shards(nx, ny, nz, spline_weights, point_source, confidence, block_dest, offsets, block_count):
    slots, points, patch = spline_weights.shape
    group = ny * nz
    cap = max(2, (slots + group - 1) // group)
    rows = 4 * cap
    vmem = pl.BlockSpec(memory_space=pltpu.VMEM)
    dma = pltpu.SemaphoreType.DMA
    hbm = pl.BlockSpec(memory_space=pltpu.HBM)
    brick = jax.ShapeDtypeStruct((BX, BY, BZ), F32)
    middle = pl.pallas_call(
        functools.partial(kernel, (nx, ny, nz, slots, cap)),
        out_shape=(
            jax.ShapeDtypeStruct((ITERS + 1, BX, BY, BZ), F32),
            jax.ShapeDtypeStruct((ITERS, slots, points), F32),
            jax.ShapeDtypeStruct((8, 128), F32),
        ),
        in_specs=[hbm] * 5 + [pl.BlockSpec(memory_space=pltpu.SMEM)],
        out_specs=(vmem, vmem, vmem),
        scratch_shapes=[
            pltpu.VMEM((group, rows, 128), F32),
            pltpu.VMEM((group, rows, 128), F32),
            pltpu.VMEM((group, cap * 128, BZ), BF16),
            pltpu.VMEM((BX, 2, BY, BZ), F32),
            pltpu.VMEM((BX // 2, 2, BY, BZ), F32),
            pltpu.VMEM((BX // 2, 2, BY, BZ), F32),
            pltpu.VMEM((BY, BZ), F32),
            pltpu.VMEM((27, BY, BZ), F32),
            pltpu.VMEM((2, BX // 2, 2, BY, BZ), F32),
            pltpu.VMEM((2, 2, 2, 2, BY, BZ), F32),
            pltpu.VMEM((2, 3, 2, BY, BZ), F32),
            pltpu.VMEM((1, 128), F32),
            pltpu.VMEM((nx * group, 1, 128), F32),
            pltpu.VMEM((1, 128), F32),
            pltpu.VMEM((nx, 1, 128), F32),
            pltpu.VMEM((group, rows, 128), F32),
            pltpu.VMEM((group, rows, 128), F32),
            pltpu.VMEM((4 * slots, 128), F32),
            pltpu.VMEM(spline_weights.shape, BF16),
            pltpu.VMEM(point_source.shape, F32),
            pltpu.VMEM(confidence.shape, F32),
            pltpu.VMEM((1, slots), jnp.int32),
            pltpu.VMEM(offsets.shape, jnp.int32),
            dma((6,)), dma((27,)), dma((27,)), dma((4,)), dma((4,)),
        ],
        compiler_params=pltpu.CompilerParams(
            collective_id=0, has_side_effects=True, vmem_limit_bytes=40 * 1024 * 1024
        ),
    )(
        *(
            pltpu.with_memory_space_constraint(a, pltpu.HBM)
            for a in (
                spline_weights, point_source, confidence, block_dest.reshape(1, slots), offsets,
            )
        ),
        block_count.reshape((1,)),
    )
    return pl.pallas_call(
        finish,
        out_shape=(brick, brick, jax.ShapeDtypeStruct((slots, points), F32)),
        in_specs=[vmem] * 3,
        out_specs=(hbm, hbm, hbm),
        scratch_shapes=[
            pltpu.VMEM((BX, BY, BZ), F32),
            pltpu.VMEM((BX, BY, BZ), F32),
            pltpu.VMEM((slots, points), F32),
            dma((3,)),
        ],
        compiler_params=pltpu.CompilerParams(vmem_limit_bytes=4 * 1024 * 1024),
    )(*middle)


def solution(mesh):
    sizes = (mesh.shape["gx"], mesh.shape["gy"], mesh.shape["gz"])
    return jax.shard_map(
        functools.partial(shards, *sizes),
        mesh=mesh,
        in_specs=(
            P(("gx", "gy", "gz"), None, None),
            P(("gx", "gy", "gz"), None),
            P(("gx", "gy", "gz"), None),
            P(("gx", "gy", "gz"), None),
            P(None, ("gx", "gy", "gz")),
            P(("gx", "gy", "gz")),
        ),
        out_specs=(P("gx", "gy", "gz"), P("gx", "gy", "gz"), P(("gx", "gy", "gz"), None)),
        check_vma=False,
    )
```

```python
import functools
import jax
import jax.numpy as jnp
from jax import lax
from jax.experimental import pallas as pl
from jax.experimental.pallas import tpu as pltpu
from jax.sharding import PartitionSpec as P

BX = 8
BY = 8
BZ = 128
PX = 4
PY = 4
PZ = 8
ITERS = 3
MESH = pl.DeviceIdType.MESH
F32 = jnp.float32
BF16 = jnp.bfloat16
HI = lax.Precision.HIGHEST
DIRS = [
    (dx, dy, dz)
    for dx in (-1, 0, 1)
    for dy in (-1, 0, 1)
    for dz in (-1, 0, 1)
    if (dx, dy, dz) != (0, 0, 0)
]


YAT = 27
XYAT = YAT + 12
XAT = XYAT + 12


def code(dx, dy, dz):
    return (dx + 1) * 9 + (dy + 1) * 3 + (dz + 1)


def halves(value):
    high = value.astype(BF16)
    return high, (value - high.astype(F32)).astype(BF16)


def iota(shape, dim):
    return lax.broadcasted_iota(jnp.int32, shape, dim)


def repeat(count, body, init):
    if count <= 8:
        for i in range(count):
            init = body(i, init)
        return init
    return lax.fori_loop(0, count, body, init)


def smooth(v):
    n = v.shape[0]
    v = v[1 : n - 1] + 0.5 * (v[: n - 2] + v[2:])
    v = v + 0.5 * (pltpu.roll(v, 1, 1) + pltpu.roll(v, 15, 1))
    return v + 0.5 * (pltpu.roll(v, 1, 2) + pltpu.roll(v, 255, 2))


def coefficients(m):
    def add(p, a, q):
        out = []
        for i in range(max(len(p), len(q))):
            left = p[i] if i < len(p) else None
            right = a * q[i] if i < len(q) else None
            out.append(right if left is None else left if right is None else left + right)
        return out

    def form(p, q):
        total = None
        for i in range(len(p)):
            for j in range(len(q)):
                term = p[i] * q[j] * m[i + j]
                total = term if total is None else total + term
        return total

    one = jnp.ones_like(m[0])
    direction, residual, field = [one], [one], []
    now = m[0]
    for step in range(ITERS):
        image = [16.0 * c for c in direction] + [jnp.zeros_like(one)]
        image = [image[i] + (16.0 * direction[i - 1] if i else 0.0) for i in range(len(image))]
        alpha = now / form(direction, image)
        field = add(field, alpha, direction)
        residual = add(residual, -alpha, image)
        if step + 1 < ITERS:
            new = form(residual, residual)
            direction = add(residual, new / now, direction)
            now = new
    return field, residual


def kernel(sizes, w_hbm, src_hbm, conf_hbm, dest_hbm, off_hbm, count_hbm,
           basis_ref, values_at, sums_ref,
           send, recv, zhot, xlow, xhigh, ylow, yhigh, zpack, halo_in,
           part, parts, colpart, colparts, back, returned, pay,
           w_ref, src_ref, conf_ref, dest_ref, off_ref, in_s, one_s, one_r):
    nx, ny, nz, slots, cap = sizes
    group = ny * nz
    gx, gy, gz = lax.axis_index("gx"), lax.axis_index("gy"), lax.axis_index("gz")
    me = gy * nz + gz

    def ring(g, n):
        return [g] + [lax.rem(g + d, n) for d in range(1, n)]

    xs, ys, zs = ring(gx, nx), ring(gy, ny), ring(gz, nz)
    in_group = [(y * nz + z, (gx, y, z)) for y in ys for z in zs][1:]
    in_column = [(x, (x, gy, gz)) for x in xs][1:]
    everyone = [((x * ny + y) * nz + z, (x, y, z)) for x in xs for y in ys for z in zs][1:]

    def spread(kind, peers, src_of, dst, slot):
        copies = []
        for other, where in peers:
            c = pltpu.make_async_remote_copy(
                src_ref=src_of(other), dst_ref=dst.at[slot], send_sem=one_s.at[kind], recv_sem=one_r.at[kind],
                device_id=where, device_id_type=MESH,
            )
            c.start()
            copies.append(c)

    def whole(kind, peers, dst):
        ref = dst.at[pl.ds(0, len(peers))]
        return pltpu.make_async_remote_copy(
            src_ref=ref, dst_ref=ref, send_sem=one_s.at[kind], recv_sem=one_r.at[kind],
            device_id=peers[0][1], device_id_type=MESH,
        )

    def exists(dx, dy, dz):
        ok = None
        for d, g, n in ((dx, gx, nx), (dy, gy, ny), (dz, gz, nz)):
            if d:
                this = g + 1 < n if d > 0 else g > 0
                ok = this if ok is None else jnp.logical_and(ok, this)
        return ok

    loads = [
        pltpu.make_async_copy(a, b, in_s.at[i])
        for i, (a, b) in enumerate(
            (
                (dest_hbm, dest_ref), (off_hbm, off_ref),
                (src_hbm, src_ref), (conf_hbm, conf_ref), (w_hbm, w_ref),
            )
        )
    ]
    barrier = pltpu.get_barrier_semaphore()
    for _, where in reversed(in_group):
        pl.semaphore_signal(barrier, inc=1, device_id=where, device_id_type=MESH)
    for c in loads:
        c.start()
    back[...] = jnp.zeros_like(back)
    halo_in[...] = jnp.zeros_like(halo_in)

    for _, where in in_column:
        pl.semaphore_signal(barrier, inc=1, device_id=where, device_id_type=MESH)

    for c in loads[:2]:
        c.wait()
    live_count = count_hbm[0]
    row_n, lane_n = iota((slots, slots), 0), iota((slots, slots), 1)
    eye = row_n == lane_n
    drow = dest_ref[...].astype(F32)
    dcol = jnp.sum(jnp.where(eye, drow, 0.0), axis=1, keepdims=True)
    earlier = (dcol == drow) & (lane_n < row_n) & (lane_n < live_count)
    rank = jnp.sum(jnp.where(earlier, 1.0, 0.0), axis=1, keepdims=True)
    tcol = jnp.where(iota((slots, 1), 0) < live_count, dcol * cap + rank, -1.0)
    off = off_ref[...].astype(F32)
    zcol = jnp.sum(jnp.where(eye, off[2:3], 0.0), axis=1, keepdims=True)
    xycol = jnp.sum(jnp.where(eye, off[0:1] * BY + off[1:2], 0.0), axis=1, keepdims=True)
    pay[2 * slots : 3 * slots, :] = jnp.broadcast_to(zcol, (slots, 128))
    pay[3 * slots : 4 * slots, :] = jnp.broadcast_to(xycol, (slots, 128))
    lanes = iota((slots, 4 * slots), 1)
    trow = jnp.sum(
        jnp.where(iota((slots, 4 * slots), 0) == lax.rem(lanes, slots), tcol, 0.0), axis=0, keepdims=True
    )
    rows = 4 * cap
    tr = iota((group * rows, 4 * slots), 0)
    tl = iota((group * rows, 4 * slots), 1)
    inner = lax.rem(tr, rows)
    want = (lax.div(tr, rows) * cap + lax.rem(inner, cap)).astype(F32)
    sel = jnp.where((lax.div(inner, cap) == lax.div(tl, slots)) & (want == trow), 1.0, 0.0)
    for c in loads[2:]:
        c.wait()
    s_hi, s_lo = halves(src_ref[...])
    c_hi, c_lo = halves(conf_ref[...])
    left_s = jnp.concatenate([s_hi, s_lo], 0)
    left_c = jnp.concatenate([c_hi, c_lo], 0)
    for n in range(slots):
        w = w_ref[n]
        wf = w.astype(F32)
        q_hi, q_lo = halves(wf * wf)
        rhs = jnp.dot(left_s, w, preferred_element_type=F32)
        den = jnp.dot(left_c, q_hi, preferred_element_type=F32) + jnp.dot(
            left_c, q_lo, preferred_element_type=F32
        )
        pay[n : n + 1, :] = rhs[n : n + 1] + rhs[slots + n : slots + n + 1]
        pay[slots + n : slots + n + 1, :] = den[n : n + 1] + den[slots + n : slots + n + 1]

    send[...] = jnp.dot(sel, pay[...], precision=HI, preferred_element_type=F32).reshape(group, rows, 128)
    recv[me] = send[me]

    pl.semaphore_wait(barrier, len(in_group) + len(in_column))
    spread(0, in_group, lambda other: send.at[other], recv, me)
    whole(0, in_group, recv).wait_recv()

    cell = iota((BX * BY, 128), 1)
    place_xy = (iota((BX * BY, 128), 0) - (lax.shift_right_logical(cell, 5) * BY + (lax.shift_right_logical(cell, 3) & 3))).astype(F32)
    place_z = (iota((128, BZ), 1) - (iota((128, BZ), 0) & 7)).astype(F32)

    def scatter(g, acc):
        got = recv[g]
        lefts, hots = [], []
        for k in range(cap):
            hot = jnp.where(place_z == got[2 * cap + k : 2 * cap + k + 1], 1.0, 0.0).astype(BF16)
            hots.append(hot)
            at = place_xy == got[3 * cap + k : 3 * cap + k + 1]
            values = jnp.concatenate(
                [jnp.where(at, got[k : k + 1], 0.0), jnp.where(at, got[cap + k : cap + k + 1], 0.0)], 0
            )
            lefts.append(jnp.concatenate(halves(values), 0))
        hot = jnp.concatenate(hots, 0)
        zhot[g] = hot
        return acc + jnp.dot(jnp.concatenate(lefts, 1), hot, preferred_element_type=F32)

    def gather_of(vectors, first):
        flat = jnp.concatenate(halves(jnp.concatenate([v.reshape(BX * BY, BZ) for v in vectors], 0)), 0)
        tall = flat.shape[0] // 2

        def gather(g, carry):
            picked = lax.dot_general(flat, zhot[g], (((1,), (1,)), ((), ())), preferred_element_type=F32)
            picked = picked[:tall] + picked[tall:]
            got = recv[g]
            at = [place_xy == got[3 * cap + k : 3 * cap + k + 1] for k in range(cap)]
            lines = []
            for v in range(len(vectors)):
                for k in range(cap):
                    cells = picked[BX * BY * v : BX * BY * (v + 1), 128 * k : 128 * k + 128]
                    lines.append(jnp.sum(jnp.where(at[k], cells, 0.0), axis=0, keepdims=True))
            back[g, first * cap : (first + len(vectors)) * cap, :] = jnp.concatenate(lines, 0)
            return carry

        repeat(group, gather, 0)

    acc = repeat(group, scatter, jnp.zeros((4 * BX * BY, BZ), F32))
    both = acc[: 2 * BX * BY] + acc[2 * BX * BY :]
    rhs = both[: BX * BY].reshape(BX, BY, BZ)
    den = (0.25 * both[BX * BY :]).reshape(BX, BY, BZ)

    lane = iota((BY, BZ), 1)
    sub = iota((BY, BZ), 0)
    rim = (lane < 3) | (lane >= BZ - 3)
    for half in range(2):
        for q in range(2):
            j = 2 * half + q
            even, odd = rhs[2 * j], pltpu.roll(rhs[2 * j + 1], 4, 0)
            ylow[3 * half + q] = jnp.where(sub < 4, even, odd)
            yhigh[3 * half + q] = jnp.where(sub < 4, odd, even)
        low, high = den[4 * half], pltpu.roll(den[4 * half], 2, 0)
        for p in range(1, 4):
            pick = lax.shift_right_logical(sub, 1) == p
            plane = den[4 * half + p]
            low = jnp.where(pick, pltpu.roll(plane, 2 * p, 0), low)
            high = jnp.where(pick, pltpu.roll(plane, (2 * p + 2) % 8, 0) if p < 3 else plane, high)
        ylow[3 * half + 2] = low
        yhigh[3 * half + 2] = high

    def buffers(dx, dy, dz):
        if dz:
            return zpack, halo_in.at[code(-dx, -dy, -dz)]
        if dy:
            source = ylow if dy < 0 else yhigh
            side = 0 if dy > 0 else 1
            if not dx:
                return source, halo_in.at[pl.ds(YAT + 6 * side, 6)]
            at = XYAT + 3 * (side if dx > 0 else 2 + side)
            return source.at[pl.ds(3 if dx > 0 else 0, 3)], halo_in.at[pl.ds(at, 3)]
        return xhigh if dx > 0 else xlow, halo_in.at[pl.ds(XAT if dx > 0 else XAT + 5, 5)]

    def halo(dx, dy, dz):
        source, target = buffers(dx, dy, dz)
        return pltpu.make_async_remote_copy(
            src_ref=source, dst_ref=target,
            send_sem=one_s.at[4], recv_sem=one_r.at[4],
            device_id=(gx + dx, gy + dy, gz + dz), device_id_type=MESH,
        )

    order = sorted(DIRS, key=lambda d: (d[2] != 0, d[1] == 0, d[0] != 0))

    def depart(directions):
        for d in directions:
            @pl.when(exists(*d))
            def _():
                halo(*d).start()

    depart([d for d in order if d[1] and not d[2]])
    for i in range(3):
        xlow[i], xhigh[i] = rhs[i], rhs[5 + i]
    for i in range(2):
        xlow[3 + i], xhigh[3 + i] = den[i], den[6 + i]
    packed = jnp.zeros((BY, BZ), F32)
    for f, field in enumerate((rhs, den)):
        for x in range(BX):
            edge = jnp.where(rim, field[x], 0.0)
            shift = 8 * x + 64 * f
            packed = packed + (pltpu.roll(edge, shift, 1) if shift else edge)
    zpack[...] = packed
    depart([d for d in order if d[2] or not d[1]])
    basis_ref[0] = rhs
    gather_of((rhs,), 0)
    whole(0, in_group, recv).wait_send()
    near = [jnp.minimum(g, 1) + jnp.minimum(n - 1 - g, 1) for g, n in ((gx, nx), (gy, ny), (gz, nz))]
    usual = [(0,) if n == 1 else (1,) if n == 2 else (1, 2) for n in (nx, ny, nz)]

    def all_halos(finish_one):
        for a in usual[0]:
            for b in usual[1]:
                for c in usual[2]:
                    tiles = 5 * a + 6 * b + 3 * a * b + c * (1 + a) * (1 + b)
                    if tiles:
                        @pl.when((near[0] == a) & (near[1] == b) & (near[2] == c))
                        def _():
                            ref = halo_in.at[pl.ds(0, tiles)]
                            finish_one(
                                pltpu.make_async_remote_copy(
                                    src_ref=ref, dst_ref=ref, send_sem=one_s.at[4], recv_sem=one_r.at[4],
                                    device_id=(gx, gy, gz), device_id_type=MESH,
                                )
                            )

    all_halos(lambda c: c.wait_recv())

    def rim_pack(dx, dy):
        return jnp.where((lane & 7) < 4, halo_in[code(dx, dy, 1)], halo_in[code(dx, dy, -1)])

    fields = [[], []]
    none = jnp.zeros((2 * BY, 2 * BZ), F32)
    for dx, xs_of in ((-1, (5, 6, 7)), (0, tuple(range(BX))), (1, (0, 1, 2))):
        pack0 = rim_pack(dx, 0)
        pack1 = jnp.where(sub < 4, rim_pack(dx, 1), rim_pack(dx, -1))
        for i, x in enumerate(xs_of):
            for f in range(2):
                if f and x == (5 if dx < 0 else 2 if dx > 0 else -1):
                    fields[f].append(none)
                    continue
                half, p = x // 4, x % 4
                at = (3 * half if dx == 0 else 0) + (2 if f else p // 2)
                if dx:
                    side = 0 if dx < 0 else 1
                    own = halo_in[XAT + 5 * side + (3 + (x % 6) if f else i)]
                    low, high = (halo_in[XYAT + 3 * (2 * side + v) + at] for v in (1, 0))
                else:
                    own = (rhs, den)[f][x]
                    low, high = halo_in[YAT + 6 + at], halo_in[YAT + at]
                if f:
                    low = pltpu.roll(low, 8 - 2 * p, 0) if p else low
                    high = pltpu.roll(high, 6 - 2 * p, 0) if p < 3 else high
                    beside = jnp.where(sub < 4, low, high)
                elif x % 2 == 0:
                    beside = jnp.where(sub < 4, low, high)
                else:
                    beside = pltpu.roll(jnp.where(sub < 4, high, low), 4, 0)
                shift = (BZ - 8 * x - 64 * f) % BZ
                z0 = jnp.where(rim, pltpu.roll(pack0, shift, 1) if shift else pack0, 0.0)
                z1 = jnp.where(rim, pltpu.roll(pack1, shift, 1) if shift else pack1, 0.0)
                top = jnp.concatenate([own, z0], 1)
                low_rows = jnp.concatenate([beside, z1], 1)
                fields[f].append(jnp.concatenate([top, low_rows], 0))
    v0, dens = jnp.stack(fields[0]), jnp.stack(fields[1])

    ry, rz = iota((16, 256), 0), iota((16, 256), 1)
    yes = ((ry < 8) | ((ry < 12) & (gy + 1 < ny)) | ((ry >= 12) & (gy > 0))) & (
        (rz < 128) | ((rz < 192) & (gz + 1 < nz)) | ((rz >= 192) & (gz > 0))
    )
    inside = jnp.where(yes, 1.0, 0.0)
    before = inside * jnp.where(gx > 0, 1.0, 0.0)
    after = inside * jnp.where(gx + 1 < nx, 1.0, 0.0)

    def step(v, depth):
        out = dens[depth : 14 - depth] * v[1:-1] - 0.125 * smooth(v)
        rims = 3 - depth
        masks = [before] * rims + [inside] * BX + [after] * rims
        return out * jnp.stack(masks) if rims else out

    v1 = step(v0, 1)
    v2 = step(v1, 2)
    v3 = step(v2, 3)
    basis = [rhs, v1[2:10, :8, :128], v2[1:9, :8, :128], v3[:, :8, :128]]
    lines = []
    for k in range(2 * ITERS):
        product = jnp.sum(basis[k // 2] * basis[(k + 1) // 2], axis=0)
        lines.append(jnp.sum(product, axis=0, keepdims=True))
    lines.append(jnp.zeros((2, 128), F32))
    fold = jnp.concatenate(lines, 0)
    for shift in (64, 32, 16):
        fold = fold + pltpu.roll(fold, shift, 1)
    own = lax.shift_right_logical(lane, 4) == sub

    direct = nx * group <= 64
    peers = everyone if direct else in_group
    spot = gx * group + me if direct else me
    line = jnp.sum(jnp.where(own, fold, 0.0), axis=0, keepdims=True)
    part[...] = line
    parts[spot] = line
    spread(1, peers, lambda other: part, parts, spot)
    for k in range(1, ITERS + 1):
        basis_ref[k] = basis[k]

    gather_of(basis[1:ITERS], 1)
    returned[me] = back[me]
    spread(2, in_group, lambda other: back.at[other], returned, me)
    all_halos(lambda c: c.wait_send())
    tr = iota((slots, group * rows), 1)
    inner = lax.rem(tr, rows)
    want = (lax.div(tr, rows) * cap + lax.rem(inner, cap)).astype(F32)
    sel = jnp.concatenate(
        [jnp.where((lax.div(inner, cap) == v) & (want == tcol), 1.0, 0.0) for v in range(ITERS)], 0
    ).astype(BF16)
    whole(2, in_group, returned).wait_recv()
    left = jnp.concatenate(
        [
            jnp.dot(sel, part_of, preferred_element_type=F32).astype(BF16)
            for part_of in halves(returned[...].reshape(group * rows, 128))
        ],
        0,
    )
    for n in range(slots):
        out = lax.dot_general(left, w_ref[n], (((1,), (1,)), ((), ())), preferred_element_type=F32)
        for v in range(ITERS):
            at = v * slots + n
            values_at[v, n : n + 1, :] = out[at : at + 1] + out[ITERS * slots + at : ITERS * slots + at + 1]

    whole(1, peers, parts).wait_recv()
    total = jnp.sum(parts[pl.ds(0, len(peers) + 1)], axis=0)
    if not direct:
        colpart[...] = total
        colparts[gx] = total
        spread(3, in_column, lambda other: colpart, colparts, gx)
        whole(3, in_column, colparts).wait_recv()
        total = jnp.sum(colparts[...], axis=0)
    sums_ref[...] = jnp.where(own, jnp.broadcast_to(total, (8, 128)), 0.0)
    whole(1, peers, parts).wait_send()
    whole(2, in_group, returned).wait_send()
    if not direct:
        whole(3, in_column, colparts).wait_send()


def finish(basis_ref, values_at, sums_ref, field_hbm, resid_hbm, point_hbm, field_ref, resid_ref, point_ref, out_s):
    moments = jnp.broadcast_to(jnp.sum(sums_ref[...], axis=1, keepdims=True), (8, 128))
    field_c, resid_c = coefficients([moments[k : k + 1] for k in range(2 * ITERS)])
    copies = [
        pltpu.make_async_copy(a, b, out_s.at[i])
        for i, (a, b) in enumerate(((field_ref, field_hbm), (point_ref, point_hbm), (resid_ref, resid_hbm)))
    ]

    def combine(cs):
        out = None
        for k, c in enumerate(cs):
            term = c.reshape(1, 1, 128) * basis_ref[k]
            out = term if out is None else out + term
        return out

    field_ref[...] = combine(field_c)
    copies[0].start()
    point = None
    for v, c in enumerate(field_c):
        term = jnp.concatenate([c] * (values_at.shape[2] // 128), 1) * values_at[v]
        point = term if point is None else point + term
    point_ref[...] = point
    copies[1].start()
    resid_ref[...] = combine(resid_c)
    copies[2].start()
    for c in copies:
        c.wait()


def shards(nx, ny, nz, spline_weights, point_source, confidence, block_dest, offsets, block_count):
    slots, points, patch = spline_weights.shape
    group = ny * nz
    cap = max(2, (slots + group - 1) // group)
    rows = 4 * cap
    vmem = pl.BlockSpec(memory_space=pltpu.VMEM)
    dma = pltpu.SemaphoreType.DMA
    hbm = pl.BlockSpec(memory_space=pltpu.HBM)
    brick = jax.ShapeDtypeStruct((BX, BY, BZ), F32)
    middle = pl.pallas_call(
        functools.partial(kernel, (nx, ny, nz, slots, cap)),
        out_shape=(
            jax.ShapeDtypeStruct((ITERS + 1, BX, BY, BZ), F32),
            jax.ShapeDtypeStruct((ITERS, slots, points), F32),
            jax.ShapeDtypeStruct((8, 128), F32),
        ),
        in_specs=[hbm] * 5 + [pl.BlockSpec(memory_space=pltpu.SMEM)],
        out_specs=(vmem, vmem, vmem),
        scratch_shapes=[
            pltpu.VMEM((group, rows, 128), F32),
            pltpu.VMEM((group, rows, 128), F32),
            pltpu.VMEM((group, cap * 128, BZ), BF16),
            pltpu.VMEM((5, BY, BZ), F32),
            pltpu.VMEM((5, BY, BZ), F32),
            pltpu.VMEM((6, BY, BZ), F32),
            pltpu.VMEM((6, BY, BZ), F32),
            pltpu.VMEM((BY, BZ), F32),
            pltpu.VMEM((XAT + 10, BY, BZ), F32),
            pltpu.VMEM((1, 128), F32),
            pltpu.VMEM((nx * group, 1, 128), F32),
            pltpu.VMEM((1, 128), F32),
            pltpu.VMEM((nx, 1, 128), F32),
            pltpu.VMEM((group, rows, 128), F32),
            pltpu.VMEM((group, rows, 128), F32),
            pltpu.VMEM((4 * slots, 128), F32),
            pltpu.VMEM(spline_weights.shape, BF16),
            pltpu.VMEM(point_source.shape, F32),
            pltpu.VMEM(confidence.shape, F32),
            pltpu.VMEM((1, slots), jnp.int32),
            pltpu.VMEM(offsets.shape, jnp.int32),
            dma((6,)), dma((5,)), dma((5,)),
        ],
        compiler_params=pltpu.CompilerParams(
            collective_id=0, has_side_effects=True, vmem_limit_bytes=40 * 1024 * 1024
        ),
    )(
        *(
            pltpu.with_memory_space_constraint(a, pltpu.HBM)
            for a in (
                spline_weights, point_source, confidence, block_dest.reshape(1, slots), offsets,
            )
        ),
        block_count.reshape((1,)),
    )
    return pl.pallas_call(
        finish,
        out_shape=(brick, brick, jax.ShapeDtypeStruct((slots, points), F32)),
        in_specs=[vmem] * 3,
        out_specs=(hbm, hbm, hbm),
        scratch_shapes=[
            pltpu.VMEM((BX, BY, BZ), F32),
            pltpu.VMEM((BX, BY, BZ), F32),
            pltpu.VMEM((slots, points), F32),
            dma((3,)),
        ],
        compiler_params=pltpu.CompilerParams(vmem_limit_bytes=4 * 1024 * 1024),
    )(*middle)


def solution(mesh):
    sizes = (mesh.shape["gx"], mesh.shape["gy"], mesh.shape["gz"])
    return jax.shard_map(
        functools.partial(shards, *sizes),
        mesh=mesh,
        in_specs=(
            P(("gx", "gy", "gz"), None, None),
            P(("gx", "gy", "gz"), None),
            P(("gx", "gy", "gz"), None),
            P(("gx", "gy", "gz"), None),
            P(None, ("gx", "gy", "gz")),
            P(("gx", "gy", "gz")),
        ),
        out_specs=(P("gx", "gy", "gz"), P("gx", "gy", "gz"), P(("gx", "gy", "gz"), None)),
        check_vma=False,
    )
```

```python
import functools
import jax
import jax.numpy as jnp
from jax import lax
from jax.experimental import pallas as pl
from jax.experimental.pallas import tpu as pltpu
from jax.sharding import PartitionSpec as P

BX = 8
BY = 8
BZ = 128
PX = 4
PY = 4
PZ = 8
ITERS = 3
MESH = pl.DeviceIdType.MESH
F32 = jnp.float32
BF16 = jnp.bfloat16
HI = lax.Precision.HIGHEST
DIRS = [
    (dx, dy, dz)
    for dx in (-1, 0, 1)
    for dy in (-1, 0, 1)
    for dz in (-1, 0, 1)
    if (dx, dy, dz) != (0, 0, 0)
]


YAT = 27
XYAT = YAT + 12
XAT = XYAT + 12


def code(dx, dy, dz):
    return (dx + 1) * 9 + (dy + 1) * 3 + (dz + 1)


def halves(value):
    high = value.astype(BF16)
    return high, (value - high.astype(F32)).astype(BF16)


def iota(shape, dim):
    return lax.broadcasted_iota(jnp.int32, shape, dim)


def repeat(count, body, init):
    if count <= 8:
        for i in range(count):
            init = body(i, init)
        return init
    return lax.fori_loop(0, count, body, init)


def smooth(v):
    n = v.shape[0]
    v = v[1 : n - 1] + 0.5 * (v[: n - 2] + v[2:])
    v = v + 0.5 * (pltpu.roll(v, 1, 1) + pltpu.roll(v, 15, 1))
    return v + 0.5 * (pltpu.roll(v, 1, 2) + pltpu.roll(v, 255, 2))


def coefficients(m):
    def add(p, a, q):
        out = []
        for i in range(max(len(p), len(q))):
            left = p[i] if i < len(p) else None
            right = a * q[i] if i < len(q) else None
            out.append(right if left is None else left if right is None else left + right)
        return out

    def form(p, q):
        total = None
        for i in range(len(p)):
            for j in range(len(q)):
                term = p[i] * q[j] * m[i + j]
                total = term if total is None else total + term
        return total

    one = jnp.ones_like(m[0])
    direction, residual, field = [one], [one], []
    now = m[0]
    for step in range(ITERS):
        image = [16.0 * c for c in direction] + [jnp.zeros_like(one)]
        image = [image[i] + (16.0 * direction[i - 1] if i else 0.0) for i in range(len(image))]
        alpha = now / form(direction, image)
        field = add(field, alpha, direction)
        residual = add(residual, -alpha, image)
        if step + 1 < ITERS:
            new = form(residual, residual)
            direction = add(residual, new / now, direction)
            now = new
    return field, residual


def kernel(sizes, w_hbm, src_hbm, conf_hbm, dest_hbm, off_hbm, count_hbm,
           basis_ref, values_at, sums_ref,
           send, recv, zhot, xlow, xhigh, ylow, yhigh, zpack, halo_in,
           part, parts, colpart, colparts, back, returned, pay,
           w_ref, src_ref, conf_ref, dest_ref, off_ref, in_s, one_s, one_r):
    nx, ny, nz, slots, cap = sizes
    group = ny * nz
    gx, gy, gz = lax.axis_index("gx"), lax.axis_index("gy"), lax.axis_index("gz")
    me = gy * nz + gz

    def ring(g, n):
        return [g] + [lax.rem(g + d, n) for d in range(1, n)]

    xs, ys, zs = ring(gx, nx), ring(gy, ny), ring(gz, nz)
    in_group = [(y * nz + z, (gx, y, z)) for y in ys for z in zs][1:]
    nearby = [(ys[y] * nz + zs[z], (gx, ys[y], zs[z])) for y in range(ny) for z in range(0, nz, 2)][1:]
    beyond = [(ys[y] * nz + zs[z], (gx, ys[y], zs[z])) for y in range(ny) for z in range(1, nz, 2)]
    in_column = [(x, (x, gy, gz)) for x in xs][1:]
    everyone = [((x * ny + y) * nz + z, (x, y, z)) for x in xs for y in ys for z in zs][1:]

    def spread(kind, peers, src_of, dst, slot):
        copies = []
        for other, where in peers:
            c = pltpu.make_async_remote_copy(
                src_ref=src_of(other), dst_ref=dst.at[slot], send_sem=one_s.at[kind], recv_sem=one_r.at[kind],
                device_id=where, device_id_type=MESH,
            )
            c.start()
            copies.append(c)

    def whole(kind, peers, dst):
        ref = dst.at[pl.ds(0, len(peers))]
        return pltpu.make_async_remote_copy(
            src_ref=ref, dst_ref=ref, send_sem=one_s.at[kind], recv_sem=one_r.at[kind],
            device_id=peers[0][1], device_id_type=MESH,
        )

    def exists(dx, dy, dz):
        ok = None
        for d, g, n in ((dx, gx, nx), (dy, gy, ny), (dz, gz, nz)):
            if d:
                this = g + 1 < n if d > 0 else g > 0
                ok = this if ok is None else jnp.logical_and(ok, this)
        return ok

    loads = [
        pltpu.make_async_copy(a, b, in_s.at[i])
        for i, (a, b) in enumerate(
            (
                (dest_hbm, dest_ref), (off_hbm, off_ref),
                (src_hbm, src_ref), (conf_hbm, conf_ref), (w_hbm, w_ref),
            )
        )
    ]
    barrier = pltpu.get_barrier_semaphore()
    for _, where in reversed(in_group):
        pl.semaphore_signal(barrier, inc=1, device_id=where, device_id_type=MESH)
    for c in loads:
        c.start()
    back[...] = jnp.zeros_like(back)
    halo_in[...] = jnp.zeros_like(halo_in)

    for _, where in in_column:
        pl.semaphore_signal(barrier, inc=1, device_id=where, device_id_type=MESH)

    for c in loads[:2]:
        c.wait()
    live_count = count_hbm[0]
    row_n, lane_n = iota((slots, slots), 0), iota((slots, slots), 1)
    eye = row_n == lane_n
    drow = dest_ref[...].astype(F32)
    dcol = jnp.sum(jnp.where(eye, drow, 0.0), axis=1, keepdims=True)
    earlier = (dcol == drow) & (lane_n < row_n) & (lane_n < live_count)
    rank = jnp.sum(jnp.where(earlier, 1.0, 0.0), axis=1, keepdims=True)
    tcol = jnp.where(iota((slots, 1), 0) < live_count, dcol * cap + rank, -1.0)
    off = off_ref[...].astype(F32)
    zcol = jnp.sum(jnp.where(eye, off[2:3], 0.0), axis=1, keepdims=True)
    xycol = jnp.sum(jnp.where(eye, off[0:1] * BY + off[1:2], 0.0), axis=1, keepdims=True)
    pay[2 * slots : 3 * slots, :] = jnp.broadcast_to(zcol, (slots, 128))
    pay[3 * slots : 4 * slots, :] = jnp.broadcast_to(xycol, (slots, 128))
    lanes = iota((slots, 4 * slots), 1)
    trow = jnp.sum(
        jnp.where(iota((slots, 4 * slots), 0) == lax.rem(lanes, slots), tcol, 0.0), axis=0, keepdims=True
    )
    rows = 4 * cap
    tr = iota((group * rows, 4 * slots), 0)
    tl = iota((group * rows, 4 * slots), 1)
    inner = lax.rem(tr, rows)
    want = (lax.div(tr, rows) * cap + lax.rem(inner, cap)).astype(F32)
    sel = jnp.where((lax.div(inner, cap) == lax.div(tl, slots)) & (want == trow), 1.0, 0.0)
    for c in loads[2:]:
        c.wait()
    s_hi, s_lo = halves(src_ref[...])
    c_hi, c_lo = halves(conf_ref[...])
    left_s = jnp.concatenate([s_hi, s_lo], 0)
    left_c = jnp.concatenate([c_hi, c_lo], 0)
    for n in range(slots):
        w = w_ref[n]
        wf = w.astype(F32)
        q_hi, q_lo = halves(wf * wf)
        rhs = jnp.dot(left_s, w, preferred_element_type=F32)
        den = jnp.dot(left_c, q_hi, preferred_element_type=F32) + jnp.dot(
            left_c, q_lo, preferred_element_type=F32
        )
        pay[n : n + 1, :] = rhs[n : n + 1] + rhs[slots + n : slots + n + 1]
        pay[slots + n : slots + n + 1, :] = den[n : n + 1] + den[slots + n : slots + n + 1]

    send[...] = jnp.dot(sel, pay[...], precision=HI, preferred_element_type=F32).reshape(group, rows, 128)
    recv[me] = send[me]

    pl.semaphore_wait(barrier, len(in_group) + len(in_column))
    spread(0, nearby, lambda other: send.at[other], recv, me)
    spread(5, beyond, lambda other: send.at[other], recv, me)

    cell = iota((BX * BY, 128), 1)
    place_xy = (iota((BX * BY, 128), 0) - (lax.shift_right_logical(cell, 5) * BY + (lax.shift_right_logical(cell, 3) & 3))).astype(F32)
    place_z = (iota((128, BZ), 1) - (iota((128, BZ), 0) & 7)).astype(F32)

    def scatter(g, acc):
        got = recv[g]
        lefts, hots = [], []
        for k in range(cap):
            hot = jnp.where(place_z == got[2 * cap + k : 2 * cap + k + 1], 1.0, 0.0).astype(BF16)
            hots.append(hot)
            at = place_xy == got[3 * cap + k : 3 * cap + k + 1]
            values = jnp.concatenate(
                [jnp.where(at, got[k : k + 1], 0.0), jnp.where(at, got[cap + k : cap + k + 1], 0.0)], 0
            )
            lefts.append(jnp.concatenate(halves(values), 0))
        hot = jnp.concatenate(hots, 0)
        zhot[g] = hot
        return acc + jnp.dot(jnp.concatenate(lefts, 1), hot, preferred_element_type=F32)

    def gather_of(vectors, first):
        flat = jnp.concatenate(halves(jnp.concatenate([v.reshape(BX * BY, BZ) for v in vectors], 0)), 0)
        tall = flat.shape[0] // 2

        def gather(g, carry):
            picked = lax.dot_general(flat, zhot[g], (((1,), (1,)), ((), ())), preferred_element_type=F32)
            picked = picked[:tall] + picked[tall:]
            got = recv[g]
            at = [place_xy == got[3 * cap + k : 3 * cap + k + 1] for k in range(cap)]
            lines = []
            for v in range(len(vectors)):
                for k in range(cap):
                    cells = picked[BX * BY * v : BX * BY * (v + 1), 128 * k : 128 * k + 128]
                    lines.append(jnp.sum(jnp.where(at[k], cells, 0.0), axis=0, keepdims=True))
            back[g, first * cap : (first + len(vectors)) * cap, :] = jnp.concatenate(lines, 0)
            return carry

        repeat(group, gather, 0)

    acc = jnp.zeros((4 * BX * BY, BZ), F32)
    if group <= 8:
        back_y, back_z = ([lax.rem(g + n - d, n) for d in range(n)] for g, n in ((gy, ny), (gz, nz)))
        for first, kind, peers_of in ((0, 0, nearby), (1, 5, beyond)):
            if peers_of:
                whole(kind, peers_of, recv).wait_recv()
            for y in range(ny):
                for z in range(first, nz, 2):
                    acc = scatter(back_y[y] * nz + back_z[z], acc)
    else:
        whole(0, nearby, recv).wait_recv()
        whole(5, beyond, recv).wait_recv()
        acc = repeat(group, scatter, acc)
    both = acc[: 2 * BX * BY] + acc[2 * BX * BY :]
    rhs = both[: BX * BY].reshape(BX, BY, BZ)
    den = (0.25 * both[BX * BY :]).reshape(BX, BY, BZ)

    lane = iota((BY, BZ), 1)
    sub = iota((BY, BZ), 0)
    rim = (lane < 3) | (lane >= BZ - 3)
    for half in range(2):
        for q in range(2):
            j = 2 * half + q
            even, odd = rhs[2 * j], pltpu.roll(rhs[2 * j + 1], 4, 0)
            ylow[3 * half + q] = jnp.where(sub < 4, even, odd)
            yhigh[3 * half + q] = jnp.where(sub < 4, odd, even)
        low, high = den[4 * half], pltpu.roll(den[4 * half], 2, 0)
        for p in range(1, 4):
            pick = lax.shift_right_logical(sub, 1) == p
            plane = den[4 * half + p]
            low = jnp.where(pick, pltpu.roll(plane, 2 * p, 0), low)
            high = jnp.where(pick, pltpu.roll(plane, (2 * p + 2) % 8, 0) if p < 3 else plane, high)
        ylow[3 * half + 2] = low
        yhigh[3 * half + 2] = high

    def buffers(dx, dy, dz):
        if dz:
            return zpack, halo_in.at[code(-dx, -dy, -dz)]
        if dy:
            source = ylow if dy < 0 else yhigh
            side = 0 if dy > 0 else 1
            if not dx:
                return source, halo_in.at[pl.ds(YAT + 6 * side, 6)]
            at = XYAT + 3 * (side if dx > 0 else 2 + side)
            return source.at[pl.ds(3 if dx > 0 else 0, 3)], halo_in.at[pl.ds(at, 3)]
        return xhigh if dx > 0 else xlow, halo_in.at[pl.ds(XAT if dx > 0 else XAT + 5, 5)]

    def halo(dx, dy, dz):
        source, target = buffers(dx, dy, dz)
        return pltpu.make_async_remote_copy(
            src_ref=source, dst_ref=target,
            send_sem=one_s.at[4], recv_sem=one_r.at[4],
            device_id=(gx + dx, gy + dy, gz + dz), device_id_type=MESH,
        )

    order = sorted(DIRS, key=lambda d: (d[2] != 0, d[1] == 0, d[0] != 0))

    def depart(directions):
        for d in directions:
            @pl.when(exists(*d))
            def _():
                halo(*d).start()

    depart([d for d in order if d[1] and not d[2]])
    for i in range(3):
        xlow[i], xhigh[i] = rhs[i], rhs[5 + i]
    for i in range(2):
        xlow[3 + i], xhigh[3 + i] = den[i], den[6 + i]
    packed = jnp.zeros((BY, BZ), F32)
    for f, field in enumerate((rhs, den)):
        for x in range(BX):
            edge = jnp.where(rim, field[x], 0.0)
            shift = 8 * x + 64 * f
            packed = packed + (pltpu.roll(edge, shift, 1) if shift else edge)
    zpack[...] = packed
    depart([d for d in order if d[2] or not d[1]])
    basis_ref[0] = rhs
    gather_of((rhs,), 0)
    whole(0, nearby, recv).wait_send()
    whole(5, beyond, recv).wait_send()
    near = [jnp.minimum(g, 1) + jnp.minimum(n - 1 - g, 1) for g, n in ((gx, nx), (gy, ny), (gz, nz))]
    usual = [(0,) if n == 1 else (1,) if n == 2 else (1, 2) for n in (nx, ny, nz)]

    def all_halos(finish_one):
        for a in usual[0]:
            for b in usual[1]:
                for c in usual[2]:
                    tiles = 5 * a + 6 * b + 3 * a * b + c * (1 + a) * (1 + b)
                    if tiles:
                        @pl.when((near[0] == a) & (near[1] == b) & (near[2] == c))
                        def _():
                            ref = halo_in.at[pl.ds(0, tiles)]
                            finish_one(
                                pltpu.make_async_remote_copy(
                                    src_ref=ref, dst_ref=ref, send_sem=one_s.at[4], recv_sem=one_r.at[4],
                                    device_id=(gx, gy, gz), device_id_type=MESH,
                                )
                            )

    all_halos(lambda c: c.wait_recv())

    def rim_pack(dx, dy):
        return jnp.where((lane & 7) < 4, halo_in[code(dx, dy, 1)], halo_in[code(dx, dy, -1)])

    fields = [[], []]
    none = jnp.zeros((2 * BY, 2 * BZ), F32)
    for dx, xs_of in ((-1, (5, 6, 7)), (0, tuple(range(BX))), (1, (0, 1, 2))):
        pack0 = rim_pack(dx, 0)
        pack1 = jnp.where(sub < 4, rim_pack(dx, 1), rim_pack(dx, -1))
        for i, x in enumerate(xs_of):
            for f in range(2):
                if f and x == (5 if dx < 0 else 2 if dx > 0 else -1):
                    fields[f].append(none)
                    continue
                half, p = x // 4, x % 4
                at = (3 * half if dx == 0 else 0) + (2 if f else p // 2)
                if dx:
                    side = 0 if dx < 0 else 1
                    own = halo_in[XAT + 5 * side + (3 + (x % 6) if f else i)]
                    low, high = (halo_in[XYAT + 3 * (2 * side + v) + at] for v in (1, 0))
                else:
                    own = (rhs, den)[f][x]
                    low, high = halo_in[YAT + 6 + at], halo_in[YAT + at]
                if f:
                    low = pltpu.roll(low, 8 - 2 * p, 0) if p else low
                    high = pltpu.roll(high, 6 - 2 * p, 0) if p < 3 else high
                    beside = jnp.where(sub < 4, low, high)
                elif x % 2 == 0:
                    beside = jnp.where(sub < 4, low, high)
                else:
                    beside = pltpu.roll(jnp.where(sub < 4, high, low), 4, 0)
                shift = (BZ - 8 * x - 64 * f) % BZ
                z0 = jnp.where(rim, pltpu.roll(pack0, shift, 1) if shift else pack0, 0.0)
                z1 = jnp.where(rim, pltpu.roll(pack1, shift, 1) if shift else pack1, 0.0)
                top = jnp.concatenate([own, z0], 1)
                low_rows = jnp.concatenate([beside, z1], 1)
                fields[f].append(jnp.concatenate([top, low_rows], 0))
    v0, dens = jnp.stack(fields[0]), jnp.stack(fields[1])

    ry, rz = iota((16, 256), 0), iota((16, 256), 1)
    yes = ((ry < 8) | ((ry < 12) & (gy + 1 < ny)) | ((ry >= 12) & (gy > 0))) & (
        (rz < 128) | ((rz < 192) & (gz + 1 < nz)) | ((rz >= 192) & (gz > 0))
    )
    inside = jnp.where(yes, 1.0, 0.0)
    before = inside * jnp.where(gx > 0, 1.0, 0.0)
    after = inside * jnp.where(gx + 1 < nx, 1.0, 0.0)

    def step(v, depth):
        out = dens[depth : 14 - depth] * v[1:-1] - 0.125 * smooth(v)
        rims = 3 - depth
        masks = [before] * rims + [inside] * BX + [after] * rims
        return out * jnp.stack(masks) if rims else out

    v1 = step(v0, 1)
    v2 = step(v1, 2)
    v3 = step(v2, 3)
    basis = [rhs, v1[2:10, :8, :128], v2[1:9, :8, :128], v3[:, :8, :128]]
    lines = []
    for k in range(2 * ITERS):
        product = jnp.sum(basis[k // 2] * basis[(k + 1) // 2], axis=0)
        lines.append(jnp.sum(product, axis=0, keepdims=True))
    lines.append(jnp.zeros((2, 128), F32))
    fold = jnp.concatenate(lines, 0)
    for shift in (64, 32, 16):
        fold = fold + pltpu.roll(fold, shift, 1)
    own = lax.shift_right_logical(lane, 4) == sub

    direct = nx * group <= 64
    peers = everyone if direct else in_group
    spot = gx * group + me if direct else me
    line = jnp.sum(jnp.where(own, fold, 0.0), axis=0, keepdims=True)
    part[...] = line
    parts[spot] = line
    spread(1, peers, lambda other: part, parts, spot)
    for k in range(1, ITERS + 1):
        basis_ref[k] = basis[k]

    gather_of(basis[1:ITERS], 1)
    returned[me] = back[me]
    spread(2, in_group, lambda other: back.at[other], returned, me)
    all_halos(lambda c: c.wait_send())
    tr = iota((slots, group * rows), 1)
    inner = lax.rem(tr, rows)
    want = (lax.div(tr, rows) * cap + lax.rem(inner, cap)).astype(F32)
    sel = jnp.concatenate(
        [jnp.where((lax.div(inner, cap) == v) & (want == tcol), 1.0, 0.0) for v in range(ITERS)], 0
    ).astype(BF16)
    whole(2, in_group, returned).wait_recv()
    left = jnp.concatenate(
        [
            jnp.dot(sel, part_of, preferred_element_type=F32).astype(BF16)
            for part_of in halves(returned[...].reshape(group * rows, 128))
        ],
        0,
    )
    for n in range(slots):
        out = lax.dot_general(left, w_ref[n], (((1,), (1,)), ((), ())), preferred_element_type=F32)
        for v in range(ITERS):
            at = v * slots + n
            values_at[v, n : n + 1, :] = out[at : at + 1] + out[ITERS * slots + at : ITERS * slots + at + 1]

    whole(1, peers, parts).wait_recv()
    total = jnp.sum(parts[pl.ds(0, len(peers) + 1)], axis=0)
    if not direct:
        colpart[...] = total
        colparts[gx] = total
        spread(3, in_column, lambda other: colpart, colparts, gx)
        whole(3, in_column, colparts).wait_recv()
        total = jnp.sum(colparts[...], axis=0)
    sums_ref[...] = jnp.where(own, jnp.broadcast_to(total, (8, 128)), 0.0)
    whole(1, peers, parts).wait_send()
    whole(2, in_group, returned).wait_send()
    if not direct:
        whole(3, in_column, colparts).wait_send()


def finish(basis_ref, values_at, sums_ref, field_hbm, resid_hbm, point_hbm, field_ref, resid_ref, point_ref, out_s):
    moments = jnp.broadcast_to(jnp.sum(sums_ref[...], axis=1, keepdims=True), (8, 128))
    field_c, resid_c = coefficients([moments[k : k + 1] for k in range(2 * ITERS)])
    copies = [
        pltpu.make_async_copy(a, b, out_s.at[i])
        for i, (a, b) in enumerate(((field_ref, field_hbm), (point_ref, point_hbm), (resid_ref, resid_hbm)))
    ]

    def combine(cs):
        out = None
        for k, c in enumerate(cs):
            term = c.reshape(1, 1, 128) * basis_ref[k]
            out = term if out is None else out + term
        return out

    field_ref[...] = combine(field_c)
    copies[0].start()
    point = None
    for v, c in enumerate(field_c):
        term = jnp.concatenate([c] * (values_at.shape[2] // 128), 1) * values_at[v]
        point = term if point is None else point + term
    point_ref[...] = point
    copies[1].start()
    resid_ref[...] = combine(resid_c)
    copies[2].start()
    for c in copies:
        c.wait()


def shards(nx, ny, nz, spline_weights, point_source, confidence, block_dest, offsets, block_count):
    slots, points, patch = spline_weights.shape
    group = ny * nz
    cap = max(2, (slots + group - 1) // group)
    rows = 4 * cap
    vmem = pl.BlockSpec(memory_space=pltpu.VMEM)
    dma = pltpu.SemaphoreType.DMA
    hbm = pl.BlockSpec(memory_space=pltpu.HBM)
    brick = jax.ShapeDtypeStruct((BX, BY, BZ), F32)
    middle = pl.pallas_call(
        functools.partial(kernel, (nx, ny, nz, slots, cap)),
        out_shape=(
            jax.ShapeDtypeStruct((ITERS + 1, BX, BY, BZ), F32),
            jax.ShapeDtypeStruct((ITERS, slots, points), F32),
            jax.ShapeDtypeStruct((8, 128), F32),
        ),
        in_specs=[hbm] * 5 + [pl.BlockSpec(memory_space=pltpu.SMEM)],
        out_specs=(vmem, vmem, vmem),
        scratch_shapes=[
            pltpu.VMEM((group, rows, 128), F32),
            pltpu.VMEM((group, rows, 128), F32),
            pltpu.VMEM((group, cap * 128, BZ), BF16),
            pltpu.VMEM((5, BY, BZ), F32),
            pltpu.VMEM((5, BY, BZ), F32),
            pltpu.VMEM((6, BY, BZ), F32),
            pltpu.VMEM((6, BY, BZ), F32),
            pltpu.VMEM((BY, BZ), F32),
            pltpu.VMEM((XAT + 10, BY, BZ), F32),
            pltpu.VMEM((1, 128), F32),
            pltpu.VMEM((nx * group, 1, 128), F32),
            pltpu.VMEM((1, 128), F32),
            pltpu.VMEM((nx, 1, 128), F32),
            pltpu.VMEM((group, rows, 128), F32),
            pltpu.VMEM((group, rows, 128), F32),
            pltpu.VMEM((4 * slots, 128), F32),
            pltpu.VMEM(spline_weights.shape, BF16),
            pltpu.VMEM(point_source.shape, F32),
            pltpu.VMEM(confidence.shape, F32),
            pltpu.VMEM((1, slots), jnp.int32),
            pltpu.VMEM(offsets.shape, jnp.int32),
            dma((6,)), dma((6,)), dma((6,)),
        ],
        compiler_params=pltpu.CompilerParams(
            collective_id=0, has_side_effects=True, vmem_limit_bytes=40 * 1024 * 1024
        ),
    )(
        *(
            pltpu.with_memory_space_constraint(a, pltpu.HBM)
            for a in (
                spline_weights, point_source, confidence, block_dest.reshape(1, slots), offsets,
            )
        ),
        block_count.reshape((1,)),
    )
    return pl.pallas_call(
        finish,
        out_shape=(brick, brick, jax.ShapeDtypeStruct((slots, points), F32)),
        in_specs=[vmem] * 3,
        out_specs=(hbm, hbm, hbm),
        scratch_shapes=[
            pltpu.VMEM((BX, BY, BZ), F32),
            pltpu.VMEM((BX, BY, BZ), F32),
            pltpu.VMEM((slots, points), F32),
            dma((3,)),
        ],
        compiler_params=pltpu.CompilerParams(vmem_limit_bytes=4 * 1024 * 1024),
    )(*middle)


def solution(mesh):
    sizes = (mesh.shape["gx"], mesh.shape["gy"], mesh.shape["gz"])
    return jax.shard_map(
        functools.partial(shards, *sizes),
        mesh=mesh,
        in_specs=(
            P(("gx", "gy", "gz"), None, None),
            P(("gx", "gy", "gz"), None),
            P(("gx", "gy", "gz"), None),
            P(("gx", "gy", "gz"), None),
            P(None, ("gx", "gy", "gz")),
            P(("gx", "gy", "gz")),
        ),
        out_specs=(P("gx", "gy", "gz"), P("gx", "gy", "gz"), P(("gx", "gy", "gz"), None)),
        check_vma=False,
    )
```

```python
import functools
import jax
import jax.numpy as jnp
from jax import lax
from jax.experimental import pallas as pl
from jax.experimental.pallas import tpu as pltpu
from jax.sharding import PartitionSpec as P

BX = 8
BY = 8
BZ = 128
PX = 4
PY = 4
PZ = 8
ITERS = 3
MESH = pl.DeviceIdType.MESH
F32 = jnp.float32
BF16 = jnp.bfloat16
HI = lax.Precision.HIGHEST
DIRS = [
    (dx, dy, dz)
    for dx in (-1, 0, 1)
    for dy in (-1, 0, 1)
    for dz in (-1, 0, 1)
    if (dx, dy, dz) != (0, 0, 0)
]


YAT = 27
XYAT = YAT + 12
XAT = XYAT + 12


def code(dx, dy, dz):
    return (dx + 1) * 9 + (dy + 1) * 3 + (dz + 1)


def halves(value):
    high = value.astype(BF16)
    return high, (value - high.astype(F32)).astype(BF16)


def iota(shape, dim):
    return lax.broadcasted_iota(jnp.int32, shape, dim)


def repeat(count, body, init):
    if count <= 8:
        for i in range(count):
            init = body(i, init)
        return init
    return lax.fori_loop(0, count, body, init)


def smooth(v):
    n = v.shape[0]
    v = v[1 : n - 1] + 0.5 * (v[: n - 2] + v[2:])
    v = v + 0.5 * (pltpu.roll(v, 1, 1) + pltpu.roll(v, 15, 1))
    return v + 0.5 * (pltpu.roll(v, 1, 2) + pltpu.roll(v, 255, 2))


def coefficients(m):
    def add(p, a, q):
        out = []
        for i in range(max(len(p), len(q))):
            left = p[i] if i < len(p) else None
            right = a * q[i] if i < len(q) else None
            out.append(right if left is None else left if right is None else left + right)
        return out

    def form(p, q):
        total = None
        for i in range(len(p)):
            for j in range(len(q)):
                term = p[i] * q[j] * m[i + j]
                total = term if total is None else total + term
        return total

    one = jnp.ones_like(m[0])
    direction, residual, field = [one], [one], []
    now = m[0]
    for step in range(ITERS):
        image = [16.0 * c for c in direction] + [jnp.zeros_like(one)]
        image = [image[i] + (16.0 * direction[i - 1] if i else 0.0) for i in range(len(image))]
        alpha = now / form(direction, image)
        field = add(field, alpha, direction)
        residual = add(residual, -alpha, image)
        if step + 1 < ITERS:
            new = form(residual, residual)
            direction = add(residual, new / now, direction)
            now = new
    return field, residual


def kernel(sizes, w_hbm, src_hbm, conf_hbm, dest_hbm, off_hbm, count_hbm,
           basis_ref, values_at, sums_ref,
           send, recv, zhot, xlow, xhigh, ylow, yhigh, zpack, halo_in,
           part, parts, colpart, colparts, back, returned, pay,
           w_ref, src_ref, conf_ref, dest_ref, off_ref, one_s, one_r):
    nx, ny, nz, slots, cap = sizes
    group = ny * nz
    gx, gy, gz = lax.axis_index("gx"), lax.axis_index("gy"), lax.axis_index("gz")
    me = gy * nz + gz

    def ring(g, n):
        return [g] + [lax.rem(g + d, n) for d in range(1, n)]

    xs, ys, zs = ring(gx, nx), ring(gy, ny), ring(gz, nz)
    in_group = [(y * nz + z, (gx, y, z)) for y in ys for z in zs][1:]
    nearby = [(ys[y] * nz + zs[z], (gx, ys[y], zs[z])) for y in range(ny) for z in range(0, nz, 2)][1:]
    beyond = [(ys[y] * nz + zs[z], (gx, ys[y], zs[z])) for y in range(ny) for z in range(1, nz, 2)]
    in_column = [(x, (x, gy, gz)) for x in xs][1:]
    everyone = [((x * ny + y) * nz + z, (x, y, z)) for x in xs for y in ys for z in zs][1:]

    def spread(kind, peers, src_of, dst, slot):
        copies = []
        for other, where in peers:
            c = pltpu.make_async_remote_copy(
                src_ref=src_of(other), dst_ref=dst.at[slot], send_sem=one_s.at[kind], recv_sem=one_r.at[kind],
                device_id=where, device_id_type=MESH,
            )
            c.start()
            copies.append(c)

    def whole(kind, peers, dst):
        ref = dst.at[pl.ds(0, len(peers))]
        return pltpu.make_async_remote_copy(
            src_ref=ref, dst_ref=ref, send_sem=one_s.at[kind], recv_sem=one_r.at[kind],
            device_id=peers[0][1], device_id_type=MESH,
        )

    def exists(dx, dy, dz):
        ok = None
        for d, g, n in ((dx, gx, nx), (dy, gy, ny), (dz, gz, nz)):
            if d:
                this = g + 1 < n if d > 0 else g > 0
                ok = this if ok is None else jnp.logical_and(ok, this)
        return ok

    loads = [
        pltpu.make_async_copy(a, b, one_s.at[i])
        for i, (a, b) in enumerate(
            (
                (dest_hbm, dest_ref), (off_hbm, off_ref),
                (src_hbm, src_ref), (conf_hbm, conf_ref), (w_hbm, w_ref),
            )
        )
    ]
    barrier = pltpu.get_barrier_semaphore()
    for _, where in beyond + nearby:
        pl.semaphore_signal(barrier, inc=1, device_id=where, device_id_type=MESH)
    for c in loads:
        c.start()
    back[...] = jnp.zeros_like(back)
    halo_in[...] = jnp.zeros_like(halo_in)

    for _, where in in_column:
        pl.semaphore_signal(barrier, inc=1, device_id=where, device_id_type=MESH)

    for c in loads[:2]:
        c.wait()
    live_count = count_hbm[0]
    row_n, lane_n = iota((slots, slots), 0), iota((slots, slots), 1)
    eye = row_n == lane_n
    drow = dest_ref[...].astype(F32)
    dcol = jnp.sum(jnp.where(eye, drow, 0.0), axis=1, keepdims=True)
    earlier = (dcol == drow) & (lane_n < row_n) & (lane_n < live_count)
    rank = jnp.sum(jnp.where(earlier, 1.0, 0.0), axis=1, keepdims=True)
    tcol = jnp.where(iota((slots, 1), 0) < live_count, dcol * cap + rank, -1.0)
    off = off_ref[...].astype(F32)
    zcol = jnp.sum(jnp.where(eye, off[2:3], 0.0), axis=1, keepdims=True)
    xycol = jnp.sum(jnp.where(eye, off[0:1] * BY + off[1:2], 0.0), axis=1, keepdims=True)
    pay[2 * slots : 3 * slots, :] = jnp.broadcast_to(zcol, (slots, 128))
    pay[3 * slots : 4 * slots, :] = jnp.broadcast_to(xycol, (slots, 128))
    lanes = iota((slots, 4 * slots), 1)
    trow = jnp.sum(
        jnp.where(iota((slots, 4 * slots), 0) == lax.rem(lanes, slots), tcol, 0.0), axis=0, keepdims=True
    )
    rows = 4 * cap
    tr = iota((group * rows, 4 * slots), 0)
    tl = iota((group * rows, 4 * slots), 1)
    inner = lax.rem(tr, rows)
    want = (lax.div(tr, rows) * cap + lax.rem(inner, cap)).astype(F32)
    sel = jnp.where((lax.div(inner, cap) == lax.div(tl, slots)) & (want == trow), 1.0, 0.0)
    for c in loads[2:]:
        c.wait()
    s_hi, s_lo = halves(src_ref[...])
    c_hi, c_lo = halves(conf_ref[...])
    left_s = jnp.concatenate([s_hi, s_lo], 0)
    left_c = jnp.concatenate([c_hi, c_lo], 0)
    for n in range(slots):
        w = w_ref[n]
        wf = w.astype(F32)
        q_hi, q_lo = halves(wf * wf)
        rhs = jnp.dot(left_s, w, preferred_element_type=F32)
        den = jnp.dot(left_c, q_hi, preferred_element_type=F32) + jnp.dot(
            left_c, q_lo, preferred_element_type=F32
        )
        pay[n : n + 1, :] = rhs[n : n + 1] + rhs[slots + n : slots + n + 1]
        pay[slots + n : slots + n + 1, :] = den[n : n + 1] + den[slots + n : slots + n + 1]

    send[...] = jnp.dot(sel, pay[...], precision=HI, preferred_element_type=F32).reshape(group, rows, 128)
    recv[me] = send[me]

    pl.semaphore_wait(barrier, len(in_group) + len(in_column))
    spread(0, nearby, lambda other: send.at[other], recv, me)
    spread(3, beyond, lambda other: send.at[other], recv, me)

    cell = iota((BX * BY, 128), 1)
    place_xy = (iota((BX * BY, 128), 0) - (lax.shift_right_logical(cell, 5) * BY + (lax.shift_right_logical(cell, 3) & 3))).astype(F32)
    place_z = (iota((128, BZ), 1) - (iota((128, BZ), 0) & 7)).astype(F32)

    def scatter(g, acc):
        got = recv[g]
        lefts, hots = [], []
        for k in range(cap):
            hot = jnp.where(place_z == got[2 * cap + k : 2 * cap + k + 1], 1.0, 0.0).astype(BF16)
            hots.append(hot)
            at = place_xy == got[3 * cap + k : 3 * cap + k + 1]
            values = jnp.concatenate(
                [jnp.where(at, got[k : k + 1], 0.0), jnp.where(at, got[cap + k : cap + k + 1], 0.0)], 0
            )
            lefts.append(jnp.concatenate(halves(values), 0))
        hot = jnp.concatenate(hots, 0)
        zhot[g] = hot
        return acc + jnp.dot(jnp.concatenate(lefts, 1), hot, preferred_element_type=F32)

    def gather_of(vectors, first):
        flat = jnp.concatenate(halves(jnp.concatenate([v.reshape(BX * BY, BZ) for v in vectors], 0)), 0)
        tall = flat.shape[0] // 2

        def gather(g, carry):
            picked = lax.dot_general(flat, zhot[g], (((1,), (1,)), ((), ())), preferred_element_type=F32)
            picked = picked[:tall] + picked[tall:]
            got = recv[g]
            at = [place_xy == got[3 * cap + k : 3 * cap + k + 1] for k in range(cap)]
            lines = []
            for v in range(len(vectors)):
                for k in range(cap):
                    cells = picked[BX * BY * v : BX * BY * (v + 1), 128 * k : 128 * k + 128]
                    lines.append(jnp.sum(jnp.where(at[k], cells, 0.0), axis=0, keepdims=True))
            back[g, first * cap : (first + len(vectors)) * cap, :] = jnp.concatenate(lines, 0)
            return carry

        repeat(group, gather, 0)

    acc = jnp.zeros((4 * BX * BY, BZ), F32)
    if group <= 8:
        back_y, back_z = ([lax.rem(g + n - d, n) for d in range(n)] for g, n in ((gy, ny), (gz, nz)))
        for first, kind, peers_of in ((0, 0, nearby), (1, 3, beyond)):
            if peers_of:
                whole(kind, peers_of, recv).wait_recv()
            for y in range(ny):
                for z in range(first, nz, 2):
                    acc = scatter(back_y[y] * nz + back_z[z], acc)
    else:
        whole(0, nearby, recv).wait_recv()
        whole(3, beyond, recv).wait_recv()
        acc = repeat(group, scatter, acc)
    both = acc[: 2 * BX * BY] + acc[2 * BX * BY :]
    rhs = both[: BX * BY].reshape(BX, BY, BZ)
    den = (0.25 * both[BX * BY :]).reshape(BX, BY, BZ)

    lane = iota((BY, BZ), 1)
    sub = iota((BY, BZ), 0)
    rim = (lane < 3) | (lane >= BZ - 3)
    for half in range(2):
        for q in range(2):
            j = 2 * half + q
            even, odd = rhs[2 * j], pltpu.roll(rhs[2 * j + 1], 4, 0)
            ylow[3 * half + q] = jnp.where(sub < 4, even, odd)
            yhigh[3 * half + q] = jnp.where(sub < 4, odd, even)
        low, high = den[4 * half], pltpu.roll(den[4 * half], 2, 0)
        for p in range(1, 4):
            pick = lax.shift_right_logical(sub, 1) == p
            plane = den[4 * half + p]
            low = jnp.where(pick, pltpu.roll(plane, 2 * p, 0), low)
            high = jnp.where(pick, pltpu.roll(plane, (2 * p + 2) % 8, 0) if p < 3 else plane, high)
        ylow[3 * half + 2] = low
        yhigh[3 * half + 2] = high

    def buffers(dx, dy, dz):
        if dz:
            return zpack, halo_in.at[code(-dx, -dy, -dz)]
        if dy:
            source = ylow if dy < 0 else yhigh
            side = 0 if dy > 0 else 1
            if not dx:
                return source, halo_in.at[pl.ds(YAT + 6 * side, 6)]
            at = XYAT + 3 * (side if dx > 0 else 2 + side)
            return source.at[pl.ds(3 if dx > 0 else 0, 3)], halo_in.at[pl.ds(at, 3)]
        return xhigh if dx > 0 else xlow, halo_in.at[pl.ds(XAT if dx > 0 else XAT + 5, 5)]

    def halo(dx, dy, dz):
        source, target = buffers(dx, dy, dz)
        return pltpu.make_async_remote_copy(
            src_ref=source, dst_ref=target,
            send_sem=one_s.at[4], recv_sem=one_r.at[4],
            device_id=(gx + dx, gy + dy, gz + dz), device_id_type=MESH,
        )

    order = sorted(DIRS, key=lambda d: (d[2] != 0, d[1] == 0, d[0] != 0))

    def depart(directions):
        for d in directions:
            @pl.when(exists(*d))
            def _():
                halo(*d).start()

    depart([d for d in order if d[1] and not d[2]])
    for i in range(3):
        xlow[i], xhigh[i] = rhs[i], rhs[5 + i]
    for i in range(2):
        xlow[3 + i], xhigh[3 + i] = den[i], den[6 + i]
    packed = jnp.zeros((BY, BZ), F32)
    for f, field in enumerate((rhs, den)):
        for x in range(BX):
            edge = jnp.where(rim, field[x], 0.0)
            shift = 8 * x + 64 * f
            packed = packed + (pltpu.roll(edge, shift, 1) if shift else edge)
    zpack[...] = packed
    depart([d for d in order if d[2] or not d[1]])
    basis_ref[0] = rhs
    gather_of((rhs,), 0)
    whole(0, nearby, recv).wait_send()
    whole(3, beyond, recv).wait_send()
    near = [jnp.minimum(g, 1) + jnp.minimum(n - 1 - g, 1) for g, n in ((gx, nx), (gy, ny), (gz, nz))]
    usual = [(0,) if n == 1 else (1,) if n == 2 else (1, 2) for n in (nx, ny, nz)]

    def all_halos(finish_one):
        for a in usual[0]:
            for b in usual[1]:
                for c in usual[2]:
                    tiles = 5 * a + 6 * b + 3 * a * b + c * (1 + a) * (1 + b)
                    if tiles:
                        @pl.when((near[0] == a) & (near[1] == b) & (near[2] == c))
                        def _():
                            ref = halo_in.at[pl.ds(0, tiles)]
                            finish_one(
                                pltpu.make_async_remote_copy(
                                    src_ref=ref, dst_ref=ref, send_sem=one_s.at[4], recv_sem=one_r.at[4],
                                    device_id=(gx, gy, gz), device_id_type=MESH,
                                )
                            )

    all_halos(lambda c: c.wait_recv())

    def rim_pack(dx, dy):
        return jnp.where((lane & 7) < 4, halo_in[code(dx, dy, 1)], halo_in[code(dx, dy, -1)])

    fields = [[], []]
    none = jnp.zeros((2 * BY, 2 * BZ), F32)
    for dx, xs_of in ((-1, (5, 6, 7)), (0, tuple(range(BX))), (1, (0, 1, 2))):
        pack0 = rim_pack(dx, 0)
        pack1 = jnp.where(sub < 4, rim_pack(dx, 1), rim_pack(dx, -1))
        for i, x in enumerate(xs_of):
            for f in range(2):
                if f and x == (5 if dx < 0 else 2 if dx > 0 else -1):
                    fields[f].append(none)
                    continue
                half, p = x // 4, x % 4
                at = (3 * half if dx == 0 else 0) + (2 if f else p // 2)
                if dx:
                    side = 0 if dx < 0 else 1
                    own = halo_in[XAT + 5 * side + (3 + (x % 6) if f else i)]
                    low, high = (halo_in[XYAT + 3 * (2 * side + v) + at] for v in (1, 0))
                else:
                    own = (rhs, den)[f][x]
                    low, high = halo_in[YAT + 6 + at], halo_in[YAT + at]
                if f:
                    low = pltpu.roll(low, 8 - 2 * p, 0) if p else low
                    high = pltpu.roll(high, 6 - 2 * p, 0) if p < 3 else high
                    beside = jnp.where(sub < 4, low, high)
                elif x % 2 == 0:
                    beside = jnp.where(sub < 4, low, high)
                else:
                    beside = pltpu.roll(jnp.where(sub < 4, high, low), 4, 0)
                shift = (BZ - 8 * x - 64 * f) % BZ
                z0 = jnp.where(rim, pltpu.roll(pack0, shift, 1) if shift else pack0, 0.0)
                z1 = jnp.where(rim, pltpu.roll(pack1, shift, 1) if shift else pack1, 0.0)
                top = jnp.concatenate([own, z0], 1)
                low_rows = jnp.concatenate([beside, z1], 1)
                fields[f].append(jnp.concatenate([top, low_rows], 0))
    v0, dens = jnp.stack(fields[0]), jnp.stack(fields[1])

    ry, rz = iota((16, 256), 0), iota((16, 256), 1)
    yes = ((ry < 8) | ((ry < 12) & (gy + 1 < ny)) | ((ry >= 12) & (gy > 0))) & (
        (rz < 128) | ((rz < 192) & (gz + 1 < nz)) | ((rz >= 192) & (gz > 0))
    )
    inside = jnp.where(yes, 1.0, 0.0)
    before = inside * jnp.where(gx > 0, 1.0, 0.0)
    after = inside * jnp.where(gx + 1 < nx, 1.0, 0.0)

    def step(v, depth):
        out = dens[depth : 14 - depth] * v[1:-1] - 0.125 * smooth(v)
        rims = 3 - depth
        masks = [before] * rims + [inside] * BX + [after] * rims
        return out * jnp.stack(masks) if rims else out

    v1 = step(v0, 1)
    v2 = step(v1, 2)
    v3 = step(v2, 3)
    basis = [rhs, v1[2:10, :8, :128], v2[1:9, :8, :128], v3[:, :8, :128]]
    lines = []
    for k in range(2 * ITERS):
        product = jnp.sum(basis[k // 2] * basis[(k + 1) // 2], axis=0)
        lines.append(jnp.sum(product, axis=0, keepdims=True))
    lines.append(jnp.zeros((2, 128), F32))
    fold = jnp.concatenate(lines, 0)
    for shift in (64, 32, 16):
        fold = fold + pltpu.roll(fold, shift, 1)
    own = lax.shift_right_logical(lane, 4) == sub

    direct = nx * group <= 64
    peers = everyone if direct else in_group
    spot = gx * group + me if direct else me
    line = jnp.sum(jnp.where(own, fold, 0.0), axis=0, keepdims=True)
    part[...] = line
    parts[spot] = line
    spread(1, peers, lambda other: part, parts, spot)
    for k in range(1, ITERS + 1):
        basis_ref[k] = basis[k]

    gather_of(basis[1:ITERS], 1)
    returned[me] = back[me]
    spread(2, in_group, lambda other: back.at[other], returned, me)
    all_halos(lambda c: c.wait_send())
    tr = iota((slots, group * rows), 1)
    inner = lax.rem(tr, rows)
    want = (lax.div(tr, rows) * cap + lax.rem(inner, cap)).astype(F32)
    sel = jnp.concatenate(
        [jnp.where((lax.div(inner, cap) == v) & (want == tcol), 1.0, 0.0) for v in range(ITERS)], 0
    ).astype(BF16)
    whole(2, in_group, returned).wait_recv()
    left = jnp.concatenate(
        [
            jnp.dot(sel, part_of, preferred_element_type=F32).astype(BF16)
            for part_of in halves(returned[...].reshape(group * rows, 128))
        ],
        0,
    )
    for n in range(slots):
        out = lax.dot_general(left, w_ref[n], (((1,), (1,)), ((), ())), preferred_element_type=F32)
        for v in range(ITERS):
            at = v * slots + n
            values_at[v, n : n + 1, :] = out[at : at + 1] + out[ITERS * slots + at : ITERS * slots + at + 1]

    whole(1, peers, parts).wait_recv()
    total = jnp.sum(parts[pl.ds(0, len(peers) + 1)], axis=0)
    if not direct:
        colpart[...] = total
        colparts[gx] = total
        spread(5, in_column, lambda other: colpart, colparts, gx)
        whole(5, in_column, colparts).wait_recv()
        total = jnp.sum(colparts[...], axis=0)
    sums_ref[...] = jnp.where(own, jnp.broadcast_to(total, (8, 128)), 0.0)
    whole(1, peers, parts).wait_send()
    whole(2, in_group, returned).wait_send()
    if not direct:
        whole(5, in_column, colparts).wait_send()


def finish(basis_ref, values_at, sums_ref, field_hbm, resid_hbm, point_hbm, field_ref, resid_ref, point_ref, out_s):
    moments = jnp.broadcast_to(jnp.sum(sums_ref[...], axis=1, keepdims=True), (8, 128))
    field_c, resid_c = coefficients([moments[k : k + 1] for k in range(2 * ITERS)])
    copies = [
        pltpu.make_async_copy(a, b, out_s.at[i])
        for i, (a, b) in enumerate(((field_ref, field_hbm), (point_ref, point_hbm), (resid_ref, resid_hbm)))
    ]

    def combine(cs):
        out = None
        for k, c in enumerate(cs):
            term = c.reshape(1, 1, 128) * basis_ref[k]
            out = term if out is None else out + term
        return out

    field_ref[...] = combine(field_c)
    copies[0].start()
    point = None
    for v, c in enumerate(field_c):
        term = jnp.concatenate([c] * (values_at.shape[2] // 128), 1) * values_at[v]
        point = term if point is None else point + term
    point_ref[...] = point
    copies[1].start()
    resid_ref[...] = combine(resid_c)
    copies[2].start()
    for c in copies:
        c.wait()


def shards(nx, ny, nz, spline_weights, point_source, confidence, block_dest, offsets, block_count):
    slots, points, patch = spline_weights.shape
    group = ny * nz
    cap = max(2, (slots + group - 1) // group)
    rows = 4 * cap
    vmem = pl.BlockSpec(memory_space=pltpu.VMEM)
    dma = pltpu.SemaphoreType.DMA
    hbm = pl.BlockSpec(memory_space=pltpu.HBM)
    brick = jax.ShapeDtypeStruct((BX, BY, BZ), F32)
    middle = pl.pallas_call(
        functools.partial(kernel, (nx, ny, nz, slots, cap)),
        out_shape=(
            jax.ShapeDtypeStruct((ITERS + 1, BX, BY, BZ), F32),
            jax.ShapeDtypeStruct((ITERS, slots, points), F32),
            jax.ShapeDtypeStruct((8, 128), F32),
        ),
        in_specs=[hbm] * 5 + [pl.BlockSpec(memory_space=pltpu.SMEM)],
        out_specs=(vmem, vmem, vmem),
        scratch_shapes=[
            pltpu.VMEM((group, rows, 128), F32),
            pltpu.VMEM((group, rows, 128), F32),
            pltpu.VMEM((group, cap * 128, BZ), BF16),
            pltpu.VMEM((5, BY, BZ), F32),
            pltpu.VMEM((5, BY, BZ), F32),
            pltpu.VMEM((6, BY, BZ), F32),
            pltpu.VMEM((6, BY, BZ), F32),
            pltpu.VMEM((BY, BZ), F32),
            pltpu.VMEM((XAT + 10, BY, BZ), F32),
            pltpu.VMEM((1, 128), F32),
            pltpu.VMEM((nx * group, 1, 128), F32),
            pltpu.VMEM((1, 128), F32),
            pltpu.VMEM((nx, 1, 128), F32),
            pltpu.VMEM((group, rows, 128), F32),
            pltpu.VMEM((group, rows, 128), F32),
            pltpu.VMEM((4 * slots, 128), F32),
            pltpu.VMEM(spline_weights.shape, BF16),
            pltpu.VMEM(point_source.shape, F32),
            pltpu.VMEM(confidence.shape, F32),
            pltpu.VMEM((1, slots), jnp.int32),
            pltpu.VMEM(offsets.shape, jnp.int32),
            dma((5 if nx * group <= 64 else 6,)), dma((5 if nx * group <= 64 else 6,)),
        ],
        compiler_params=pltpu.CompilerParams(
            collective_id=0, has_side_effects=True, vmem_limit_bytes=40 * 1024 * 1024
        ),
    )(
        *(
            pltpu.with_memory_space_constraint(a, pltpu.HBM)
            for a in (
                spline_weights, point_source, confidence, block_dest.reshape(1, slots), offsets,
            )
        ),
        block_count.reshape((1,)),
    )
    return pl.pallas_call(
        finish,
        out_shape=(brick, brick, jax.ShapeDtypeStruct((slots, points), F32)),
        in_specs=[vmem] * 3,
        out_specs=(hbm, hbm, hbm),
        scratch_shapes=[
            pltpu.VMEM((BX, BY, BZ), F32),
            pltpu.VMEM((BX, BY, BZ), F32),
            pltpu.VMEM((slots, points), F32),
            dma((3,)),
        ],
        compiler_params=pltpu.CompilerParams(vmem_limit_bytes=4 * 1024 * 1024),
    )(*middle)


def solution(mesh):
    sizes = (mesh.shape["gx"], mesh.shape["gy"], mesh.shape["gz"])
    return jax.shard_map(
        functools.partial(shards, *sizes),
        mesh=mesh,
        in_specs=(
            P(("gx", "gy", "gz"), None, None),
            P(("gx", "gy", "gz"), None),
            P(("gx", "gy", "gz"), None),
            P(("gx", "gy", "gz"), None),
            P(None, ("gx", "gy", "gz")),
            P(("gx", "gy", "gz")),
        ),
        out_specs=(P("gx", "gy", "gz"), P("gx", "gy", "gz"), P(("gx", "gy", "gz"), None)),
        check_vma=False,
    )
```

```python
import functools
import jax
import jax.numpy as jnp
from jax import lax
from jax.experimental import pallas as pl
from jax.experimental.pallas import tpu as pltpu
from jax.sharding import PartitionSpec as P

BX = 8
BY = 8
BZ = 128
PX = 4
PY = 4
PZ = 8
ITERS = 3
MESH = pl.DeviceIdType.MESH
F32 = jnp.float32
BF16 = jnp.bfloat16
HI = lax.Precision.HIGHEST
DIRS = [
    (dx, dy, dz)
    for dx in (-1, 0, 1)
    for dy in (-1, 0, 1)
    for dz in (-1, 0, 1)
    if (dx, dy, dz) != (0, 0, 0)
]


YAT = 27
XYAT = YAT + 12
XAT = XYAT + 12


def code(dx, dy, dz):
    return (dx + 1) * 9 + (dy + 1) * 3 + (dz + 1)


def halves(value):
    high = value.astype(BF16)
    return high, (value - high.astype(F32)).astype(BF16)


def iota(shape, dim):
    return lax.broadcasted_iota(jnp.int32, shape, dim)


def repeat(count, body, init):
    if count <= 8:
        for i in range(count):
            init = body(i, init)
        return init
    return lax.fori_loop(0, count, body, init)


def smooth(v):
    n = v.shape[0]
    v = v[1 : n - 1] + 0.5 * (v[: n - 2] + v[2:])
    v = v + 0.5 * (pltpu.roll(v, 1, 1) + pltpu.roll(v, 15, 1))
    return v + 0.5 * (pltpu.roll(v, 1, 2) + pltpu.roll(v, 255, 2))


def coefficients(m):
    def add(p, a, q):
        out = []
        for i in range(max(len(p), len(q))):
            left = p[i] if i < len(p) else None
            right = a * q[i] if i < len(q) else None
            out.append(right if left is None else left if right is None else left + right)
        return out

    def form(p, q):
        total = None
        for i in range(len(p)):
            for j in range(len(q)):
                term = p[i] * q[j] * m[i + j]
                total = term if total is None else total + term
        return total

    one = jnp.ones_like(m[0])
    direction, residual, field = [one], [one], []
    now = m[0]
    for step in range(ITERS):
        image = [16.0 * c for c in direction] + [jnp.zeros_like(one)]
        image = [image[i] + (16.0 * direction[i - 1] if i else 0.0) for i in range(len(image))]
        alpha = now / form(direction, image)
        field = add(field, alpha, direction)
        residual = add(residual, -alpha, image)
        if step + 1 < ITERS:
            new = form(residual, residual)
            direction = add(residual, new / now, direction)
            now = new
    return field, residual


def kernel(sizes, w_hbm, src_hbm, conf_hbm, dest_hbm, off_hbm, count_hbm,
           basis_ref, values_at, sums_ref,
           send, recv, zhot, xlow, xhigh, ylow, yhigh, zpack, halo_in,
           part, parts, colpart, colparts, back, returned, pay,
           w_ref, src_ref, conf_ref, dest_ref, off_ref, one_s, one_r):
    nx, ny, nz, slots, cap = sizes
    group = ny * nz
    gx, gy, gz = lax.axis_index("gx"), lax.axis_index("gy"), lax.axis_index("gz")
    me = gy * nz + gz

    def ring(g, n):
        return [g] + [lax.rem(g + d, n) for d in range(1, n)]

    xs, ys, zs = ring(gx, nx), ring(gy, ny), ring(gz, nz)
    in_group = [(y * nz + z, (gx, y, z)) for y in ys for z in zs][1:]
    nearby = [(ys[y] * nz + zs[z], (gx, ys[y], zs[z])) for y in range(ny) for z in range(0, nz, 2)][1:]
    beyond = [(ys[y] * nz + zs[z], (gx, ys[y], zs[z])) for y in range(ny) for z in range(1, nz, 2)]
    in_column = [(x, (x, gy, gz)) for x in xs][1:]
    everyone = [((x * ny + y) * nz + z, (x, y, z)) for x in xs for y in ys for z in zs][1:]

    def spread(kind, peers, src_of, dst, slot):
        copies = []
        for other, where in peers:
            c = pltpu.make_async_remote_copy(
                src_ref=src_of(other), dst_ref=dst.at[slot], send_sem=one_s.at[kind], recv_sem=one_r.at[kind],
                device_id=where, device_id_type=MESH,
            )
            c.start()
            copies.append(c)

    def whole(kind, peers, dst):
        ref = dst.at[pl.ds(0, len(peers))]
        return pltpu.make_async_remote_copy(
            src_ref=ref, dst_ref=ref, send_sem=one_s.at[kind], recv_sem=one_r.at[kind],
            device_id=peers[0][1], device_id_type=MESH,
        )

    def exists(dx, dy, dz):
        ok = None
        for d, g, n in ((dx, gx, nx), (dy, gy, ny), (dz, gz, nz)):
            if d:
                this = g + 1 < n if d > 0 else g > 0
                ok = this if ok is None else jnp.logical_and(ok, this)
        return ok

    loads = [
        pltpu.make_async_copy(a, b, one_s.at[i])
        for i, (a, b) in enumerate(
            (
                (dest_hbm, dest_ref), (off_hbm, off_ref),
                (src_hbm, src_ref), (conf_hbm, conf_ref), (w_hbm, w_ref),
            )
        )
    ]
    barrier = pltpu.get_barrier_semaphore()
    for _, where in beyond + nearby:
        pl.semaphore_signal(barrier, inc=1, device_id=where, device_id_type=MESH)
    for c in loads:
        c.start()
    back[...] = jnp.zeros_like(back)
    halo_in[...] = jnp.zeros_like(halo_in)

    for _, where in in_column:
        pl.semaphore_signal(barrier, inc=1, device_id=where, device_id_type=MESH)

    for c in loads[:2]:
        c.wait()
    live_count = count_hbm[0]
    row_n, lane_n = iota((slots, slots), 0), iota((slots, slots), 1)
    eye = row_n == lane_n
    drow = dest_ref[...].astype(F32)
    dcol = jnp.sum(jnp.where(eye, drow, 0.0), axis=1, keepdims=True)
    earlier = (dcol == drow) & (lane_n < row_n) & (lane_n < live_count)
    rank = jnp.sum(jnp.where(earlier, 1.0, 0.0), axis=1, keepdims=True)
    tcol = jnp.where(iota((slots, 1), 0) < live_count, dcol * cap + rank, -1.0)
    off = off_ref[...].astype(F32)
    zcol = jnp.sum(jnp.where(eye, off[2:3], 0.0), axis=1, keepdims=True)
    xycol = jnp.sum(jnp.where(eye, off[0:1] * BY + off[1:2], 0.0), axis=1, keepdims=True)
    pay[2 * slots : 3 * slots, :] = jnp.broadcast_to(zcol, (slots, 128))
    pay[3 * slots : 4 * slots, :] = jnp.broadcast_to(xycol, (slots, 128))
    lanes = iota((slots, 4 * slots), 1)
    trow = jnp.sum(
        jnp.where(iota((slots, 4 * slots), 0) == lax.rem(lanes, slots), tcol, 0.0), axis=0, keepdims=True
    )
    rows = 4 * cap
    tr = iota((group * rows, 4 * slots), 0)
    tl = iota((group * rows, 4 * slots), 1)
    inner = lax.rem(tr, rows)
    want = (lax.div(tr, rows) * cap + lax.rem(inner, cap)).astype(F32)
    sel = jnp.where((lax.div(inner, cap) == lax.div(tl, slots)) & (want == trow), 1.0, 0.0)
    for c in loads[2:]:
        c.wait()
    s_hi, s_lo = halves(src_ref[...])
    c_hi, c_lo = halves(conf_ref[...])
    left_s = jnp.concatenate([s_hi, s_lo], 0)
    left_c = jnp.concatenate([c_hi, c_lo], 0)
    for n in range(slots):
        w = w_ref[n]
        wf = w.astype(F32)
        q_hi, q_lo = halves(wf * wf)
        rhs = jnp.dot(left_s, w, preferred_element_type=F32)
        den = jnp.dot(left_c, q_hi, preferred_element_type=F32) + jnp.dot(
            left_c, q_lo, preferred_element_type=F32
        )
        pay[n : n + 1, :] = rhs[n : n + 1] + rhs[slots + n : slots + n + 1]
        pay[slots + n : slots + n + 1, :] = den[n : n + 1] + den[slots + n : slots + n + 1]

    send[...] = jnp.dot(sel, pay[...], precision=HI, preferred_element_type=F32).reshape(group, rows, 128)
    recv[me] = send[me]

    pl.semaphore_wait(barrier, len(in_group) + len(in_column))
    spread(0, nearby, lambda other: send.at[other], recv, me)
    spread(3, beyond, lambda other: send.at[other], recv, me)

    cell = iota((BX * BY, 128), 1)
    place_xy = (iota((BX * BY, 128), 0) - (lax.shift_right_logical(cell, 5) * BY + (lax.shift_right_logical(cell, 3) & 3))).astype(F32)
    place_z = (iota((128, BZ), 1) - (iota((128, BZ), 0) & 7)).astype(F32)

    def scatter(g, acc):
        got = recv[g]
        lefts, hots = [], []
        for k in range(cap):
            hot = jnp.where(place_z == got[2 * cap + k : 2 * cap + k + 1], 1.0, 0.0).astype(BF16)
            hots.append(hot)
            at = place_xy == got[3 * cap + k : 3 * cap + k + 1]
            values = jnp.concatenate(
                [jnp.where(at, got[k : k + 1], 0.0), jnp.where(at, got[cap + k : cap + k + 1], 0.0)], 0
            )
            lefts.append(jnp.concatenate(halves(values), 0))
        hot = jnp.concatenate(hots, 0)
        zhot[g] = hot
        return acc + jnp.dot(jnp.concatenate(lefts, 1), hot, preferred_element_type=F32)

    def gather_of(vectors, first):
        flat = jnp.concatenate(halves(jnp.concatenate([v.reshape(BX * BY, BZ) for v in vectors], 0)), 0)
        tall = flat.shape[0] // 2

        def gather(g, carry):
            picked = lax.dot_general(flat, zhot[g], (((1,), (1,)), ((), ())), preferred_element_type=F32)
            picked = picked[:tall] + picked[tall:]
            got = recv[g]
            at = [place_xy == got[3 * cap + k : 3 * cap + k + 1] for k in range(cap)]
            lines = []
            for v in range(len(vectors)):
                for k in range(cap):
                    cells = picked[BX * BY * v : BX * BY * (v + 1), 128 * k : 128 * k + 128]
                    lines.append(jnp.sum(jnp.where(at[k], cells, 0.0), axis=0, keepdims=True))
            back[g, first * cap : (first + len(vectors)) * cap, :] = jnp.concatenate(lines, 0)
            return carry

        repeat(group, gather, 0)

    acc = jnp.zeros((4 * BX * BY, BZ), F32)
    if group <= 8:
        back_y, back_z = ([lax.rem(g + n - d, n) for d in range(n)] for g, n in ((gy, ny), (gz, nz)))
        for first, kind, peers_of in ((0, 0, nearby), (1, 3, beyond)):
            if peers_of:
                whole(kind, peers_of, recv).wait_recv()
            for y in range(ny):
                for z in range(first, nz, 2):
                    acc = scatter(back_y[y] * nz + back_z[z], acc)
    else:
        whole(0, nearby, recv).wait_recv()
        whole(3, beyond, recv).wait_recv()
        acc = repeat(group, scatter, acc)
    both = acc[: 2 * BX * BY] + acc[2 * BX * BY :]
    rhs = both[: BX * BY].reshape(BX, BY, BZ)
    den = (0.25 * both[BX * BY :]).reshape(BX, BY, BZ)

    lane = iota((BY, BZ), 1)
    sub = iota((BY, BZ), 0)
    rim = (lane < 3) | (lane >= BZ - 3)
    for half in range(2):
        for q in range(2):
            j = 2 * half + q
            even, odd = rhs[2 * j], pltpu.roll(rhs[2 * j + 1], 4, 0)
            ylow[3 * half + q] = jnp.where(sub < 4, even, odd)
            yhigh[3 * half + q] = jnp.where(sub < 4, odd, even)
        low, high = den[4 * half], pltpu.roll(den[4 * half], 2, 0)
        for p in range(1, 4):
            pick = lax.shift_right_logical(sub, 1) == p
            plane = den[4 * half + p]
            low = jnp.where(pick, pltpu.roll(plane, 2 * p, 0), low)
            high = jnp.where(pick, pltpu.roll(plane, (2 * p + 2) % 8, 0) if p < 3 else plane, high)
        ylow[3 * half + 2] = low
        yhigh[3 * half + 2] = high

    def buffers(dx, dy, dz):
        if dz:
            return zpack, halo_in.at[code(-dx, -dy, -dz)]
        if dy:
            source = ylow if dy < 0 else yhigh
            side = 0 if dy > 0 else 1
            if not dx:
                return source, halo_in.at[pl.ds(YAT + 6 * side, 6)]
            at = XYAT + 3 * (side if dx > 0 else 2 + side)
            return source.at[pl.ds(3 if dx > 0 else 0, 3)], halo_in.at[pl.ds(at, 3)]
        return xhigh if dx > 0 else xlow, halo_in.at[pl.ds(XAT if dx > 0 else XAT + 5, 5)]

    def halo(dx, dy, dz):
        source, target = buffers(dx, dy, dz)
        return pltpu.make_async_remote_copy(
            src_ref=source, dst_ref=target,
            send_sem=one_s.at[4], recv_sem=one_r.at[4],
            device_id=(gx + dx, gy + dy, gz + dz), device_id_type=MESH,
        )

    order = sorted(DIRS, key=lambda d: (d[2] != 0, d[1] == 0, d[0] != 0))

    def depart(directions):
        for d in directions:
            @pl.when(exists(*d))
            def _():
                halo(*d).start()

    depart([d for d in order if d[1] and not d[2]])
    for i in range(3):
        xlow[i], xhigh[i] = rhs[i], rhs[5 + i]
    for i in range(2):
        xlow[3 + i], xhigh[3 + i] = den[i], den[6 + i]
    packed = jnp.zeros((BY, BZ), F32)
    for f, field in enumerate((rhs, den)):
        for x in range(BX):
            edge = jnp.where(rim, field[x], 0.0)
            shift = 8 * x + 64 * f
            packed = packed + (pltpu.roll(edge, shift, 1) if shift else edge)
    zpack[...] = packed
    depart([d for d in order if d[2] or not d[1]])
    basis_ref[0] = rhs
    gather_of((rhs,), 0)
    whole(0, nearby, recv).wait_send()
    whole(3, beyond, recv).wait_send()
    near = [jnp.minimum(g, 1) + jnp.minimum(n - 1 - g, 1) for g, n in ((gx, nx), (gy, ny), (gz, nz))]
    usual = [(0,) if n == 1 else (1,) if n == 2 else (1, 2) for n in (nx, ny, nz)]

    def all_halos(finish_one):
        for a in usual[0]:
            for b in usual[1]:
                for c in usual[2]:
                    tiles = 5 * a + 6 * b + 3 * a * b + c * (1 + a) * (1 + b)
                    if tiles:
                        @pl.when((near[0] == a) & (near[1] == b) & (near[2] == c))
                        def _():
                            ref = halo_in.at[pl.ds(0, tiles)]
                            finish_one(
                                pltpu.make_async_remote_copy(
                                    src_ref=ref, dst_ref=ref, send_sem=one_s.at[4], recv_sem=one_r.at[4],
                                    device_id=(gx, gy, gz), device_id_type=MESH,
                                )
                            )

    all_halos(lambda c: c.wait_recv())

    def rim_pack(dx, dy):
        return jnp.where((lane & 7) < 4, halo_in[code(dx, dy, 1)], halo_in[code(dx, dy, -1)])

    fields = [[], []]
    none = jnp.zeros((2 * BY, 2 * BZ), F32)
    for dx, xs_of in ((-1, (5, 6, 7)), (0, tuple(range(BX))), (1, (0, 1, 2))):
        pack0 = rim_pack(dx, 0)
        pack1 = jnp.where(sub < 4, rim_pack(dx, 1), rim_pack(dx, -1))
        for i, x in enumerate(xs_of):
            for f in range(2):
                if f and x == (5 if dx < 0 else 2 if dx > 0 else -1):
                    fields[f].append(none)
                    continue
                half, p = x // 4, x % 4
                at = (3 * half if dx == 0 else 0) + (2 if f else p // 2)
                if dx:
                    side = 0 if dx < 0 else 1
                    own = halo_in[XAT + 5 * side + (3 + (x % 6) if f else i)]
                    low, high = (halo_in[XYAT + 3 * (2 * side + v) + at] for v in (1, 0))
                else:
                    own = (rhs, den)[f][x]
                    low, high = halo_in[YAT + 6 + at], halo_in[YAT + at]
                if f:
                    low = pltpu.roll(low, 8 - 2 * p, 0) if p else low
                    high = pltpu.roll(high, 6 - 2 * p, 0) if p < 3 else high
                    beside = jnp.where(sub < 4, low, high)
                elif x % 2 == 0:
                    beside = jnp.where(sub < 4, low, high)
                else:
                    beside = pltpu.roll(jnp.where(sub < 4, high, low), 4, 0)
                shift = (BZ - 8 * x - 64 * f) % BZ
                z0 = jnp.where(rim, pltpu.roll(pack0, shift, 1) if shift else pack0, 0.0)
                z1 = jnp.where(rim, pltpu.roll(pack1, shift, 1) if shift else pack1, 0.0)
                top = jnp.concatenate([own, z0], 1)
                low_rows = jnp.concatenate([beside, z1], 1)
                fields[f].append(jnp.concatenate([top, low_rows], 0))
    v0, dens = jnp.stack(fields[0]), jnp.stack(fields[1])

    ry, rz = iota((16, 256), 0), iota((16, 256), 1)
    yes = ((ry < 8) | ((ry < 12) & (gy + 1 < ny)) | ((ry >= 12) & (gy > 0))) & (
        (rz < 128) | ((rz < 192) & (gz + 1 < nz)) | ((rz >= 192) & (gz > 0))
    )
    inside = jnp.where(yes, 1.0, 0.0)
    before = inside * jnp.where(gx > 0, 1.0, 0.0)
    after = inside * jnp.where(gx + 1 < nx, 1.0, 0.0)

    def step(v, depth):
        out = dens[depth : 14 - depth] * v[1:-1] - 0.125 * smooth(v)
        rims = 3 - depth
        masks = [before] * rims + [inside] * BX + [after] * rims
        return out * jnp.stack(masks) if rims else out

    v1 = step(v0, 1)
    v2 = step(v1, 2)
    v3 = step(v2, 3)
    basis = [rhs, v1[2:10, :8, :128], v2[1:9, :8, :128], v3[:, :8, :128]]
    lines = []
    for k in range(2 * ITERS):
        product = jnp.sum(basis[k // 2] * basis[(k + 1) // 2], axis=0)
        lines.append(jnp.sum(product, axis=0, keepdims=True))
    lines.append(jnp.zeros((2, 128), F32))
    fold = jnp.concatenate(lines, 0)
    for shift in (64, 32, 16):
        fold = fold + pltpu.roll(fold, shift, 1)
    own = lax.shift_right_logical(lane, 4) == sub

    direct = nx * group <= 64
    peers = everyone if direct else in_group
    spot = gx * group + me if direct else me
    line = jnp.sum(jnp.where(own, fold, 0.0), axis=0, keepdims=True)
    part[...] = line
    parts[spot] = line
    spread(1, peers, lambda other: part, parts, spot)
    for k in range(1, ITERS + 1):
        basis_ref[k] = basis[k]

    gather_of(basis[1:ITERS], 1)
    returned[me] = back[me]
    spread(2, in_group, lambda other: back.at[other], returned, me)
    all_halos(lambda c: c.wait_send())
    tr = iota((slots, group * rows), 1)
    inner = lax.rem(tr, rows)
    want = (lax.div(tr, rows) * cap + lax.rem(inner, cap)).astype(F32)
    sel = jnp.concatenate(
        [jnp.where((lax.div(inner, cap) == v) & (want == tcol), 1.0, 0.0) for v in range(ITERS)], 0
    ).astype(BF16)
    whole(2, in_group, returned).wait_recv()
    left = jnp.concatenate(
        [
            jnp.dot(sel, part_of, preferred_element_type=F32).astype(BF16)
            for part_of in halves(returned[...].reshape(group * rows, 128))
        ],
        0,
    )
    for n in range(slots):
        out = lax.dot_general(left, w_ref[n], (((1,), (1,)), ((), ())), preferred_element_type=F32)
        for v in range(ITERS):
            at = v * slots + n
            values_at[v, n : n + 1, :] = out[at : at + 1] + out[ITERS * slots + at : ITERS * slots + at + 1]

    whole(1, peers, parts).wait_send()
    whole(2, in_group, returned).wait_send()
    whole(1, peers, parts).wait_recv()
    total = jnp.sum(parts[pl.ds(0, len(peers) + 1)], axis=0)
    if not direct:
        colpart[...] = total
        colparts[gx] = total
        spread(5, in_column, lambda other: colpart, colparts, gx)
        whole(5, in_column, colparts).wait_recv()
        total = jnp.sum(colparts[...], axis=0)
    sums_ref[...] = jnp.where(own, jnp.broadcast_to(total, (8, 128)), 0.0)
    if not direct:
        whole(5, in_column, colparts).wait_send()


def finish(basis_ref, values_at, sums_ref, field_hbm, resid_hbm, point_hbm, field_ref, resid_ref, point_ref, out_s):
    moments = jnp.broadcast_to(jnp.sum(sums_ref[...], axis=1, keepdims=True), (8, 128))
    field_c, resid_c = coefficients([moments[k : k + 1] for k in range(2 * ITERS)])
    copies = [
        pltpu.make_async_copy(a, b, out_s.at[i])
        for i, (a, b) in enumerate(((field_ref, field_hbm), (point_ref, point_hbm), (resid_ref, resid_hbm)))
    ]

    def combine(cs):
        out = None
        for k, c in enumerate(cs):
            term = c.reshape(1, 1, 128) * basis_ref[k]
            out = term if out is None else out + term
        return out

    field_ref[...] = combine(field_c)
    point = None
    for v, c in enumerate(field_c):
        term = jnp.concatenate([c] * (values_at.shape[2] // 128), 1) * values_at[v]
        point = term if point is None else point + term
    point_ref[...] = point
    resid_ref[...] = combine(resid_c)
    for c in copies:
        c.start()
    for c in copies:
        c.wait()


def shards(nx, ny, nz, spline_weights, point_source, confidence, block_dest, offsets, block_count):
    slots, points, patch = spline_weights.shape
    group = ny * nz
    cap = max(2, (slots + group - 1) // group)
    rows = 4 * cap
    vmem = pl.BlockSpec(memory_space=pltpu.VMEM)
    dma = pltpu.SemaphoreType.DMA
    hbm = pl.BlockSpec(memory_space=pltpu.HBM)
    brick = jax.ShapeDtypeStruct((BX, BY, BZ), F32)
    middle = pl.pallas_call(
        functools.partial(kernel, (nx, ny, nz, slots, cap)),
        out_shape=(
            jax.ShapeDtypeStruct((ITERS + 1, BX, BY, BZ), F32),
            jax.ShapeDtypeStruct((ITERS, slots, points), F32),
            jax.ShapeDtypeStruct((8, 128), F32),
        ),
        in_specs=[hbm] * 5 + [pl.BlockSpec(memory_space=pltpu.SMEM)],
        out_specs=(vmem, vmem, vmem),
        scratch_shapes=[
            pltpu.VMEM((group, rows, 128), F32),
            pltpu.VMEM((group, rows, 128), F32),
            pltpu.VMEM((group, cap * 128, BZ), BF16),
            pltpu.VMEM((5, BY, BZ), F32),
            pltpu.VMEM((5, BY, BZ), F32),
            pltpu.VMEM((6, BY, BZ), F32),
            pltpu.VMEM((6, BY, BZ), F32),
            pltpu.VMEM((BY, BZ), F32),
            pltpu.VMEM((XAT + 10, BY, BZ), F32),
            pltpu.VMEM((1, 128), F32),
            pltpu.VMEM((nx * group, 1, 128), F32),
            pltpu.VMEM((1, 128), F32),
            pltpu.VMEM((nx, 1, 128), F32),
            pltpu.VMEM((group, rows, 128), F32),
            pltpu.VMEM((group, rows, 128), F32),
            pltpu.VMEM((4 * slots, 128), F32),
            pltpu.VMEM(spline_weights.shape, BF16),
            pltpu.VMEM(point_source.shape, F32),
            pltpu.VMEM(confidence.shape, F32),
            pltpu.VMEM((1, slots), jnp.int32),
            pltpu.VMEM(offsets.shape, jnp.int32),
            dma((5 if nx * group <= 64 else 6,)), dma((5 if nx * group <= 64 else 6,)),
        ],
        compiler_params=pltpu.CompilerParams(
            collective_id=0, has_side_effects=True, vmem_limit_bytes=40 * 1024 * 1024
        ),
    )(
        *(
            pltpu.with_memory_space_constraint(a, pltpu.HBM)
            for a in (
                spline_weights, point_source, confidence, block_dest.reshape(1, slots), offsets,
            )
        ),
        block_count.reshape((1,)),
    )
    return pl.pallas_call(
        finish,
        out_shape=(brick, brick, jax.ShapeDtypeStruct((slots, points), F32)),
        in_specs=[vmem] * 3,
        out_specs=(hbm, hbm, hbm),
        scratch_shapes=[
            pltpu.VMEM((BX, BY, BZ), F32),
            pltpu.VMEM((BX, BY, BZ), F32),
            pltpu.VMEM((slots, points), F32),
            dma((3,)),
        ],
        compiler_params=pltpu.CompilerParams(vmem_limit_bytes=4 * 1024 * 1024),
    )(*middle)


def solution(mesh):
    sizes = (mesh.shape["gx"], mesh.shape["gy"], mesh.shape["gz"])
    return jax.shard_map(
        functools.partial(shards, *sizes),
        mesh=mesh,
        in_specs=(
            P(("gx", "gy", "gz"), None, None),
            P(("gx", "gy", "gz"), None),
            P(("gx", "gy", "gz"), None),
            P(("gx", "gy", "gz"), None),
            P(None, ("gx", "gy", "gz")),
            P(("gx", "gy", "gz")),
        ),
        out_specs=(P("gx", "gy", "gz"), P("gx", "gy", "gz"), P(("gx", "gy", "gz"), None)),
        check_vma=False,
    )
```
